128 devices in a mesh: sec: 32 (over x, y, z_hi), tile: 4 (over z_lo, core).
Axes of the slice: x: 4, y: 4, z: 4 (z_hi: 2, z_lo: 2; z = z_hi * 2 + z_lo), core: 2. Of those that a mesh axis runs over, the one named last changes fastest.
Arguments:
- features: bfloat16 [96, 32, 64, 128], P('sec', None, 'tile'), may hold values from -6 to 6
- vote_grad: float32 [96, 2, 64, 128], P('sec', None, 'tile'), may hold values from -6 to 6
- sharpness: float32 [96], P('sec')
- valid_rows: int32 [96], P('sec'), may hold values from 32 to 64
- first_kernel: bfloat16 [3, 3, 64, 64], replicated, may hold values from -0.25 to 0.25
- first_bias: float32 [64], replicated, may hold values from -3 to 3
- second_kernel: bfloat16 [3, 3, 2, 64], replicated, may hold values from -0.25 to 0.25
- second_bias: float32 [2], replicated, may hold values from -3 to 3
Outputs:
- voted_field: float32 [96, 2, 64, 128], P('sec', None, 'tile')
- feature_grad: float32 [96, 32, 64, 128], P('sec', None, 'tile')
The draws below stay inside these ranges and needn't reach their ends.
All inputs are finite; a program needn't handle non-finite values.
Results may differ from the reference program's by a relative error of at most 0.03.
Values may be sent and summed in bfloat16 or wider, within the bound.
No kernel may reach another device: no remote copies, remote signals or barrier semaphores. Data moves between devices by JAX's collectives and lax.ppermute only.
A program may use at most 128 MiB of HBM per device.

```python
import jax
import jax.numpy as jnp
from jax import lax

C = 32
HID = 64
COLS = 128
ROWS = 64
SECTIONS = 96


def draw_sharpness(key, part):
    key = jax.random.fold_in(key, 7)
    return jnp.exp(jax.random.uniform(key, (SECTIONS,), jnp.float32, jnp.log(0.5), jnp.log(8.0)))


def set_ends(values, rng, low, high):
    extent = values.shape
    spot = [jax.random.randint(jax.random.fold_in(rng, axis), (), 0, extent[axis]) for axis in range(len(extent))]
    values = values.at[tuple(spot)].set(low)
    longest = extent.index(max(extent))
    spot[longest] = (spot[longest] + 1) % extent[longest]
    return values.at[tuple(spot)].set(high)


def block_scale(own_key, shape, split, least, high):
    gain, own = 1.0, jax.random.fold_in(own_key, 6)
    for dim, shards_of in split:
        steps = jnp.exp(jax.random.uniform(jax.random.fold_in(own, dim), (shards_of,), jnp.float32, least / len(split), high / len(split)))
        gain = gain * jnp.repeat(steps, shape[dim] // shards_of).reshape([-1 if axis == dim else 1 for axis in range(len(shape))])
    return gain


def noise(own_key, extent, width, most, cuts=(), kind=jnp.bfloat16):
    drawn = jax.random.normal(own_key, extent, jnp.float32) * width
    if len(cuts) > 0:
        drawn = block_scale(own_key, extent, cuts, -0.22, 0.18) * drawn
    return jnp.clip(drawn, min=-most, max=most).astype(kind)


def setup_inputs(seed: int = 0) -> dict:
    arg_keys = jax.random.split(jax.random.key(seed), 9)
    features = noise(arg_keys[0], (SECTIONS, C, ROWS, COLS), 1.0, 6.0, ((0, 32), (2, 4)))
    vote_grad = noise(arg_keys[1], (SECTIONS, 2, ROWS, COLS), 1.0, 6.0, ((0, 32), (2, 4)), jnp.float32)
    sharpness = draw_sharpness(jax.random.fold_in(arg_keys[8], 71), 0)
    valid_rows = set_ends(jax.random.randint(arg_keys[3], (SECTIONS,), ROWS // 2, ROWS + 1), jax.random.fold_in(arg_keys[3], 1), ROWS // 2, ROWS).astype(jnp.int32)
    first_kernel = noise(arg_keys[4], (3, 3, HID, 2 * C), (18 * C) ** -0.5, 0.25)
    first_bias = noise(arg_keys[5], (HID,), 0.5, 3.0, (), jnp.float32)
    second_kernel = noise(arg_keys[6], (3, 3, 2, HID), (9 * HID) ** -0.5, 0.25)
    second_bias = noise(arg_keys[7], (2,), 1.0, 3.0, (), jnp.float32)
    return dict(features=features, vote_grad=vote_grad, sharpness=sharpness, valid_rows=valid_rows, first_kernel=first_kernel, first_bias=first_bias, second_kernel=second_kernel, second_bias=second_bias)


def convolve(inputs, kernel, bias):
    rows = inputs.shape[2] - 2
    cols = inputs.shape[3]
    padded = jnp.pad(inputs, ((0, 0), (0, 0), (0, 0), (1, 1)))
    total = jnp.zeros((inputs.shape[0], kernel.shape[2], rows, cols), jnp.float32)
    for shift_row in range(3):
        for shift_col in range(3):
            window = padded[:, :, shift_row:shift_row + rows, shift_col:shift_col + cols]
            total = total + jnp.einsum('oc,nchw->nohw', kernel[shift_row, shift_col], window, preferred_element_type=jnp.float32)
    return total + bias[None, :, None, None]

def predict(feat, sharp, row_start, margin, total_rows, first_kernel, first_bias, second_kernel, second_bias):
    count = feat.shape[0] - 3
    rows = feat.shape[2]
    hidden_pos = row_start - margin + 1 + jnp.arange(rows - 2, dtype=jnp.int32)
    keep = ((hidden_pos >= 0) & (hidden_pos < total_rows)).astype(jnp.float32)
    fields = []
    for lag in (1, 2, 3):
        current = feat[3:].astype(jnp.bfloat16)
        earlier = feat[3 - lag:3 - lag + count].astype(jnp.bfloat16)
        paired = jnp.concatenate([current, earlier], axis=1)
        hidden = jax.nn.relu(convolve(paired, first_kernel, first_bias)) * keep[None, None, :, None]
        hidden = hidden.astype(jnp.bfloat16)
        fields.append(convolve(hidden, second_kernel, second_bias))
    stacked = jnp.stack(fields)
    scores = []
    for k in range(3):
        acc = jnp.zeros(stacked.shape[1:2] + stacked.shape[3:], jnp.float32)
        for j in range(3):
            diff = stacked[k] - stacked[j]
            acc = acc + lax.optimization_barrier(jnp.sum(diff * diff, axis=1))
        scores.append(acc)
    logits = -sharp[None, :, None, None] * jnp.stack(scores)
    top = lax.optimization_barrier(jnp.max(logits, axis=0, keepdims=True))
    expo = jnp.exp(logits - top)
    weights = expo / lax.optimization_barrier(jnp.sum(expo, axis=0, keepdims=True))
    return lax.optimization_barrier(jnp.sum(weights[:, :, None] * stacked, axis=0))

def reference(features, vote_grad, sharpness, valid_rows, first_kernel, first_bias, second_kernel, second_bias):
    feat = jnp.pad(features.astype(jnp.float32), ((3, 0), (0, 0), (2, 2), (0, 0)))
    positions = jnp.arange(ROWS, dtype=jnp.int32)
    zero = jnp.zeros((), jnp.int32)

    def one(acc, index):
        index = index.astype(jnp.int32)
        window = lax.dynamic_slice(feat, (index, zero, zero, zero), (4,) + feat.shape[1:])
        sharp = lax.dynamic_slice(sharpness, (index,), (1,))
        valid = lax.dynamic_slice(valid_rows, (index,), (1,))
        cot = lax.dynamic_slice(vote_grad, (index, zero, zero, zero), (1,) + vote_grad.shape[1:])
        mask = (positions[None, :] < valid[:, None]).astype(jnp.float32)
        cot = cot * mask[:, None, :, None]
        vote, pull = jax.vjp(lambda f: predict(f, sharp, 0, 2, ROWS, first_kernel, first_bias, second_kernel, second_bias), window)
        grad, = pull(cot)
        old = lax.dynamic_slice(acc, (index, zero, zero, zero), grad.shape)
        acc = lax.dynamic_update_slice(acc, old + grad, (index, zero, zero, zero))
        return (acc, vote[0])
    start = jnp.zeros(feat.shape, jnp.float32)
    acc, votes = lax.scan(one, start, jnp.arange(SECTIONS, dtype=jnp.int32))
    return (votes, acc[3:, :, 2:2 + ROWS])
```

```python
import jax
import jax.numpy as jnp
from jax import lax
from jax.experimental import pallas as pl
from jax.experimental.pallas import tpu as pltpu
from jax.sharding import PartitionSpec as P

F32 = jnp.float32
BF16 = jnp.bfloat16
OWN = 3
CH = 32
HID = 64
TR = 16
COLS = 128
HALO = 4
FEAT_ROWS = TR + 2 * HALO
HID_ROWS = FEAT_ROWS - 2
FLD_ROWS = FEAT_ROWS - 4
DH_ROWS = FEAT_ROWS - 6
EDGE = HALO * OWN * CH
EDGE_ALL = EDGE + 32


def lane(shape):
    return lax.broadcasted_iota(jnp.int32, shape, len(shape) - 1)


def from_left(x):
    return jnp.where(lane(x.shape) == 0, 0.0, pltpu.roll(x, 1, x.ndim - 1))


def from_right(x):
    return jnp.where(lane(x.shape) == COLS - 1, 0.0, pltpu.roll(x, COLS - 1, x.ndim - 1))


def dot(a, b):
    return jnp.dot(a, b, preferred_element_type=F32)


def edges_kernel(info, valid, feat, vgrad, top, bottom, wide, ext):
    row0 = info[0]
    for out, first, cot_first in ((top, 0, 0), (bottom, TR - HALO, TR - 2)):
        ext[...] = jnp.zeros((32, COLS), F32)
        for s in range(OWN):
            pos = row0 + cot_first + lax.broadcasted_iota(jnp.int32, (2, COLS), 0)
            for c in range(2):
                cot = jnp.where(pos < valid[s], vgrad[s, c, cot_first : cot_first + 2, :], 0.0)
                high = cot.astype(BF16).astype(F32)
                at = s * 4 + c * 2
                ext[at : at + 2, :] = high
                ext[12 + at : 14 + at, :] = cot - high
        out[EDGE:, :] = ext[...].astype(BF16)
    for s in range(OWN):
        wide[...] = feat[s].astype(F32)
        for out, first in ((top, 0), (bottom, TR - HALO)):
            for r in range(HALO):
                at = (r * OWN + s) * CH
                out[at : at + CH, :] = wide[:, first + r, :].astype(BF16)


def edges(info, valid, feat, vgrad):
    smem = pl.BlockSpec(memory_space=pltpu.SMEM)
    vmem = pl.BlockSpec(memory_space=pltpu.VMEM)
    shape = jax.ShapeDtypeStruct((EDGE_ALL, COLS), BF16)
    return pl.pallas_call(
        edges_kernel,
        out_shape=(shape, shape),
        in_specs=[smem, smem, vmem, vmem],
        out_specs=(vmem, vmem),
        scratch_shapes=[pltpu.VMEM((CH, TR, COLS), F32), pltpu.VMEM((32, COLS), F32)],
        name="edges",
    )(info, valid, feat, vgrad)


def spread_row(x, xd, j, r):
    xd[j, r, 0:CH, :] = from_left(x).astype(BF16)
    xd[j, r, CH : 2 * CH, :] = x.astype(BF16)
    xd[j, r, 2 * CH :, :] = from_right(x).astype(BF16)


def spread(feat, above, below, keep, has_above, has_below, xd, j0, wide):
    for s in range(OWN):
        wide[s] = feat[s].astype(F32) * keep
    scale_above = keep * has_above
    scale_below = keep * has_below
    for s in range(OWN):
        for r in range(TR):
            spread_row(wide[s, :, r, :], xd, j0 + s, HALO + r)
        for r in range(HALO):
            at = (r * OWN + s) * CH
            spread_row(above[at : at + CH, :].astype(F32) * scale_above, xd, j0 + s, r)
            spread_row(
                below[at : at + CH, :].astype(F32) * scale_below, xd, j0 + s, HALO + TR + r
            )


def taps(ref, rows, pick):
    return jnp.concatenate(
        [jnp.concatenate([pick(ref, r), pick(ref, r + 1)], axis=1) for r in rows], axis=0
    )


def hidden_stage(row0, xd, wcur, wear, wboth, bias, w2f, hid, tsum):
    def step(i, carry):
        r = 2 * i
        pos = row0 - 3 + r
        keep = jnp.concatenate(
            [
                jnp.full((HID, COLS), ((pos + d >= 0) & (pos + d < 4 * TR)).astype(F32))
                for d in range(2)
            ],
            axis=1,
        )
        cur, ear = {}, {}
        for j in range(6):
            rhs = taps(xd, (r, r + 1, r + 2), lambda ref, q, j=j: ref[j, q])
            if j < 3:
                ear[j] = dot(wear[...], rhs)
            elif j < 5:
                both = dot(wboth[...], rhs)
                cur[j] = both[:HID] + bias[...]
                ear[j] = both[HID:]
            else:
                cur[j] = dot(wcur[...], rhs) + bias[...]
        for s in range(OWN):
            parts = []
            for k in (1, 2, 3):
                h = jnp.maximum(cur[3 + s] + ear[3 + s - k], 0.0) * keep
                parts.append(h.astype(BF16))
            h3 = jnp.concatenate(parts, axis=0)
            hid[r, 192 * s : 192 * s + 192, :] = h3[:, :COLS]
            hid[r + 1, 192 * s : 192 * s + 192, :] = h3[:, COLS:]
            t = dot(w2f[...], h3)
            tsum[s, r] = t[:, :COLS]
            tsum[s, r + 1] = t[:, COLS:]
        return carry

    lax.fori_loop(0, HID_ROWS // 2, step, 0)


def vote_stage(row0, sharp, valid, vgrad, above, below, has, bias2, tsum, fld, cot, grd, g3, voted):
    ends = [
        (above[EDGE:, :].astype(F32) * has[0], 0),
        (below[EDGE:, :].astype(F32) * has[1], TR + 2),
    ]
    for s in range(OWN):
        for c in range(2):
            at = s * 4 + c * 2
            for ext, first in ends:
                cot[s, c, first : first + 2, :] = ext[at : at + 2] + ext[12 + at : 14 + at]
            pos = row0 + lax.broadcasted_iota(jnp.int32, (TR, COLS), 0)
            cot[s, c, 2 : 2 + TR, :] = jnp.where(pos < valid[s], vgrad[s, c], 0.0)

    def field_row(r, carry):
        for s in range(OWN):
            sums = []
            for dx in range(3):
                acc = tsum[s, r, 8 * dx : 8 * dx + 8, :]
                for dy in (1, 2):
                    at = 8 * (3 * dy + dx)
                    acc = acc + tsum[s, r + dy, at : at + 8, :]
                sums.append(acc)
            fld[s, r] = sums[1] + from_left(sums[0]) + from_right(sums[2]) + bias2[...]
        return carry

    lax.fori_loop(0, FLD_ROWS, field_row, 0, unroll=2)

    for s in range(OWN):
        f = [[fld[s, :, 2 * k + c, :] for c in range(2)] for k in range(3)]
        beta = sharp[s]
        diff = {}
        dist = {}
        for a, b in ((0, 1), (0, 2), (1, 2)):
            diff[a, b] = [f[a][c] - f[b][c] for c in range(2)]
            dist[a, b] = diff[a, b][0] * diff[a, b][0] + diff[a, b][1] * diff[a, b][1]
        score = [dist[0, 1] + dist[0, 2], dist[0, 1] + dist[1, 2], dist[0, 2] + dist[1, 2]]
        logit = [-beta * q for q in score]
        top = jnp.maximum(jnp.maximum(logit[0], logit[1]), logit[2])
        expo = [jnp.exp(q - top) for q in logit]
        inv = 1.0 / (expo[0] + expo[1] + expo[2])
        w = [q * inv for q in expo]
        v = [w[0] * f[0][c] + w[1] * f[1][c] + w[2] * f[2][c] for c in range(2)]
        for c in range(2):
            voted[s, c] = v[c][2 : 2 + TR]
        g = [cot[s, c, 0:FLD_ROWS, :] for c in range(2)]
        e = [
            -beta * w[k] * (g[0] * (f[k][0] - v[0]) + g[1] * (f[k][1] - v[1])) for k in range(3)
        ]
        pair = {key: 2.0 * (e[key[0]] + e[key[1]]) for key in diff}
        for c in range(2):
            m01 = pair[0, 1] * diff[0, 1][c]
            m02 = pair[0, 2] * diff[0, 2][c]
            m12 = pair[1, 2] * diff[1, 2][c]
            grd[s, :, 0 + c, :] = w[0] * g[c] + m01 + m02
            grd[s, :, 2 + c, :] = w[1] * g[c] - m01 + m12
            grd[s, :, 4 + c, :] = w[2] * g[c] - m02 - m12
        grd[s, :, 6, :] = jnp.zeros((FLD_ROWS, COLS), F32)
        grd[s, :, 7, :] = jnp.zeros((FLD_ROWS, COLS), F32)

    def spread_grad(r, carry):
        for s in range(OWN):
            x = grd[s, r]
            g3[s, r] = jnp.concatenate(
                [from_right(x), x, from_left(x), jnp.zeros_like(x)], axis=0
            ).astype(BF16)
        return carry

    lax.fori_loop(0, FLD_ROWS, spread_grad, 0, unroll=2)


def hidden_grad_stage(w2b, g3, hid, dlow, down):
    def step(i, carry):
        q = 2 * i
        masked = {}
        for s in range(OWN):
            rhs = taps(g3, (q + 2, q + 1, q), lambda ref, r, s=s: ref[s, r])
            dh = dot(w2b[...], rhs)
            h = jnp.concatenate(
                [hid[q + 2 + d, 192 * s : 192 * s + 192, :] for d in range(2)], axis=1
            )
            dh = jnp.where(h.astype(F32) > 0.0, dh, 0.0)
            for k in (1, 2, 3):
                masked[s, k] = dh[HID * (k - 1) : HID * k]
        low = jnp.concatenate(
            [
                masked[0, 3],
                masked[0, 2] + masked[1, 3],
                masked[0, 1] + masked[1, 2] + masked[2, 3],
            ],
            axis=0,
        ).astype(BF16)
        cur = [masked[s, 1] + masked[s, 2] + masked[s, 3] for s in range(OWN)]
        own = jnp.concatenate(
            [cur[0], masked[1, 1] + masked[2, 2], cur[1], masked[2, 1], cur[2]], axis=0
        ).astype(BF16)
        for d in range(2):
            dlow[q + d] = low[:, COLS * d : COLS * d + COLS]
            down[q + d] = own[:, COLS * d : COLS * d + COLS]
        return carry

    lax.fori_loop(0, DH_ROWS // 2, step, 0)


def gather_columns(p):
    return from_right(p[:CH]) + p[CH : 2 * CH] + from_left(p[2 * CH :])


def feature_grad_stage(dref, jobs):
    def step(i, carry):
        r = 2 * i
        for first, size, weight, out, s in jobs:
            rhs = taps(
                dref,
                (r + 2, r + 1, r),
                lambda ref, q, first=first, size=size: ref[q, first : first + size, :],
            )
            p = dot(weight[...], rhs)
            for d in range(2):
                out[r + d, s] = gather_columns(p[:, COLS * d : COLS * d + COLS]).astype(out.dtype)
        return carry

    lax.fori_loop(0, TR // 2, step, 0)


def main_kernel(
    info, valid, sharp,
    feat, prev, above, below, pabove, pbelow, vgrad,
    wcur, wear, wboth, bias, w2f, bias2, w2b, wgcur, wgear, wgboth,
    voted, low, own,
    wide, xd, hid, tsum, fld, cot, grd, g3, dlow, down,
):
    row0 = info[0]
    has = [(info[1] > 0).astype(F32), (info[2] > 0).astype(F32)]
    keep_prev = (info[3] > 0).astype(F32)
    spread(feat, above, below, 1.0, has[0], has[1], xd, 3, wide)
    spread(prev, pabove, pbelow, keep_prev, has[0], has[1], xd, 0, wide)
    hidden_stage(row0, xd, wcur, wear, wboth, bias, w2f, hid, tsum)
    vote_stage(
        row0, sharp, valid, vgrad, above, below, has, bias2, tsum, fld, cot, grd, g3, voted
    )
    hidden_grad_stage(w2b, g3, hid, dlow, down)
    feature_grad_stage(dlow, [(64 * s, 64, wgear, low, s) for s in range(OWN)])
    feature_grad_stage(
        down, [(0, 128, wgboth, own, 0), (128, 128, wgboth, own, 1), (256, 64, wgcur, own, 2)]
    )


def main(*args):
    smem = pl.BlockSpec(memory_space=pltpu.SMEM)
    vmem = pl.BlockSpec(memory_space=pltpu.VMEM)
    return pl.pallas_call(
        main_kernel,
        out_shape=(
            jax.ShapeDtypeStruct((OWN, 2, TR, COLS), F32),
            jax.ShapeDtypeStruct((TR, OWN, CH, COLS), BF16),
            jax.ShapeDtypeStruct((TR, OWN, CH, COLS), F32),
        ),
        in_specs=[smem] * 3 + [vmem] * (len(args) - 3),
        out_specs=(vmem, vmem, vmem),
        scratch_shapes=[
            pltpu.VMEM((OWN, CH, TR, COLS), F32),
            pltpu.VMEM((6, FEAT_ROWS, 3 * CH, COLS), BF16),
            pltpu.VMEM((HID_ROWS, 9 * HID, COLS), BF16),
            pltpu.VMEM((OWN, HID_ROWS, 72, COLS), F32),
            pltpu.VMEM((OWN, FLD_ROWS, 8, COLS), F32),
            pltpu.VMEM((OWN, 2, 24, COLS), F32),
            pltpu.VMEM((OWN, FLD_ROWS, 8, COLS), F32),
            pltpu.VMEM((OWN, FLD_ROWS, 32, COLS), BF16),
            pltpu.VMEM((DH_ROWS, 3 * HID, COLS), BF16),
            pltpu.VMEM((DH_ROWS, 5 * HID, COLS), BF16),
        ],
        compiler_params=pltpu.CompilerParams(vmem_limit_bytes=40 << 20),
        name="main",
    )(*args)


def finish_kernel(info, own, back, out):
    keep = (info[4] > 0).astype(F32)

    def step(r, carry):
        for s in range(OWN):
            out[s, :, r, :] = own[r, s] + back[r, s].astype(F32) * keep
        return carry

    for r in range(TR):
        step(r, 0)


def finish(info, own, back):
    smem = pl.BlockSpec(memory_space=pltpu.SMEM)
    vmem = pl.BlockSpec(memory_space=pltpu.VMEM)
    return pl.pallas_call(
        finish_kernel,
        out_shape=jax.ShapeDtypeStruct((OWN, CH, TR, COLS), F32),
        in_specs=[smem, vmem, vmem],
        out_specs=vmem,
        name="finish",
    )(info, own, back)


def shift(value, secs, tiles):
    n, m = lax.axis_size("sec"), lax.axis_size("tile")
    pairs = [
        (a * m + b, ((a + secs) % n) * m + (b + tiles) % m) for a in range(n) for b in range(m)
    ]
    return lax.ppermute(value, ("sec", "tile"), pairs)


def body(
    features, vote_grad, sharpness, valid_rows, first_kernel, first_bias, second_kernel, second_bias
):
    sec, tile = lax.axis_index("sec"), lax.axis_index("tile")
    info = jnp.stack(
        [tile * TR, tile, lax.axis_size("tile") - 1 - tile, sec, lax.axis_size("sec") - 1 - sec]
    ).astype(jnp.int32)

    prev = shift(features, 1, 0)
    top, bottom = edges(info, valid_rows, features, vote_grad)
    above = shift(bottom, 0, 1)
    below = shift(top, 0, -1)
    pabove = shift(bottom, 1, 1)
    pbelow = shift(top, 1, -1)

    k1 = first_kernel
    forward = k1.transpose(2, 0, 1, 3)
    wcur = forward[..., :CH].reshape(HID, 9 * CH)
    wear = forward[..., CH:].reshape(HID, 9 * CH)
    wboth = jnp.concatenate([wcur, wear], axis=0)
    backward = k1.transpose(1, 3, 0, 2)
    wgcur = backward[:, :CH].reshape(3 * CH, 3 * HID)
    wgear = backward[:, CH:].reshape(3 * CH, 3 * HID)
    wgboth = jnp.stack([backward[:, :CH], backward[:, CH:]], axis=3).reshape(3 * CH, 6 * HID)
    eye = jnp.eye(4, 3, dtype=BF16)
    w2 = second_kernel[:, :, None, :, None, :] * eye[None, None, :, None, :, None]
    w2f = w2.reshape(72, 3 * HID)
    w2b = jnp.pad(w2.reshape(3, 24, 3 * HID), ((0, 0), (0, 8), (0, 0))).reshape(96, 3 * HID).T
    bias = first_bias[:, None]
    bias2 = jnp.tile(second_bias, 4)[:, None]

    voted, low, own = main(
        info, valid_rows, sharpness,
        features, prev, above, below, pabove, pbelow, vote_grad,
        wcur, wear, wboth, bias, w2f, bias2, w2b, wgcur, wgear, wgboth,
    )
    back = shift(low, -1, 0)
    return (voted, finish(info, own, back))


def solution(mesh):
    return jax.shard_map(
        body,
        mesh=mesh,
        in_specs=(
            P("sec", None, "tile", None),
            P("sec", None, "tile", None),
            P("sec"),
            P("sec"),
            P(),
            P(),
            P(),
            P(),
        ),
        out_specs=(P("sec", None, "tile", None), P("sec", None, "tile", None)),
        check_vma=False,
    )
```

```python
import jax
import jax.numpy as jnp
from jax import lax
from jax.experimental import pallas as pl
from jax.experimental.pallas import tpu as pltpu
from jax.sharding import PartitionSpec as P

F32 = jnp.float32
BF16 = jnp.bfloat16
OWN = 3
CH = 32
HID = 64
TR = 16
COLS = 128
HALO = 4
FEAT_ROWS = TR + 2 * HALO
HID_ROWS = FEAT_ROWS - 2
FLD_ROWS = FEAT_ROWS - 4
DH_ROWS = FEAT_ROWS - 6
EDGE = HALO * OWN * CH
EDGE_ALL = EDGE + 32


def lane(shape):
    return lax.broadcasted_iota(jnp.int32, shape, len(shape) - 1)


def from_left(x):
    return jnp.where(lane(x.shape) == 0, 0.0, pltpu.roll(x, 1, x.ndim - 1))


def from_right(x):
    return jnp.where(lane(x.shape) == COLS - 1, 0.0, pltpu.roll(x, COLS - 1, x.ndim - 1))


def dot(a, b):
    return jnp.dot(a, b, preferred_element_type=F32)


def params(mib):
    return pltpu.CompilerParams(vmem_limit_bytes=mib << 20)


def call(kernel, outs, scratch, mib, name, scalars, *args):
    smem = pl.BlockSpec(memory_space=pltpu.SMEM)
    vmem = pl.BlockSpec(memory_space=pltpu.VMEM)
    return pl.pallas_call(
        kernel,
        out_shape=tuple(jax.ShapeDtypeStruct(shape, kind) for shape, kind in outs),
        in_specs=[smem] * scalars + [vmem] * (len(args) - scalars),
        out_specs=(vmem,) * len(outs),
        scratch_shapes=[pltpu.VMEM(shape, kind) for shape, kind in scratch],
        compiler_params=params(mib),
        cost_estimate=pl.CostEstimate(flops=0, bytes_accessed=0, transcendentals=0),
        name=name,
    )(*args)


def first_row():
    return lax.axis_index("tile") * TR


def has_tiles():
    tile = lax.axis_index("tile")
    return (tile > 0).astype(F32), (tile < lax.axis_size("tile") - 1).astype(F32)


def edges_kernel(valid, feat, vgrad, top, bottom, wide, ext):
    row0 = first_row()
    for out, cot_first in ((top, 0), (bottom, TR - 2)):
        ext[...] = jnp.zeros((32, COLS), F32)
        for s in range(OWN):
            pos = row0 + cot_first + lax.broadcasted_iota(jnp.int32, (2, COLS), 0)
            for c in range(2):
                cot = jnp.where(pos < valid[s], vgrad[s, c, cot_first : cot_first + 2, :], 0.0)
                high = cot.astype(BF16).astype(F32)
                at = s * 4 + c * 2
                ext[at : at + 2, :] = high
                ext[12 + at : 14 + at, :] = cot - high
        out[EDGE:, :] = ext[...].astype(BF16)
    for s in range(OWN):
        wide[s] = feat[s].astype(F32)
    for s in range(OWN):
        for out, first in ((top, 0), (bottom, TR - HALO)):
            for r in range(HALO):
                at = (r * OWN + s) * CH
                out[at : at + CH, :] = wide[s, :, first + r, :].astype(BF16)


def edges(valid, feat, vgrad):
    return call(
        edges_kernel,
        [((EDGE_ALL, COLS), BF16)] * 2,
        [((OWN, CH, TR, COLS), F32), ((32, COLS), F32)],
        4,
        "edges",
        1,
        valid,
        feat,
        vgrad,
    )


def weights_kernel(
    k1, k2, wcur, wear, wboth, w2own, w2first, w2rest, w2b, w2brest, wgear, wgcur, wgboth,
    fwd, bwd, both, two, sq,
):
    for dy in range(3):
        for dx in range(3):
            k = k1[dy, dx].astype(F32)
            t = CH * (3 * dy + dx)
            fwd[0:HID, t : t + CH] = k[:, :CH]
            fwd[HID:, t : t + CH] = k[:, CH:]
            kt = k.T
            rows = slice(CH * dx, CH * dx + CH)
            bwd[rows, HID * dy : HID * dy + HID] = kt[:CH]
            bwd[3 * CH + CH * dx : 4 * CH + CH * dx, HID * dy : HID * dy + HID] = kt[CH:]
            both[rows, 2 * HID * dy : 2 * HID * dy + HID] = kt[:CH]
            both[rows, 2 * HID * dy + HID : 2 * HID * dy + 2 * HID] = kt[CH:]
    wcur[...] = fwd[0:HID, :].astype(BF16)
    wear[...] = fwd[HID:, :].astype(BF16)
    wboth[...] = fwd[...].astype(BF16)
    wgcur[...] = bwd[0 : 3 * CH, :].astype(BF16)
    wgear[...] = bwd[3 * CH :, :].astype(BF16)
    wgboth[...] = both[...].astype(BF16)

    def put(ref, row, col, lags):
        for i, lag in enumerate(lags):
            for dy in range(3):
                for dx in range(3):
                    at = row + 8 * (3 * dy + dx) + 2 * lag
                    c = col + HID * i
                    ref[at : at + 2, c : c + HID] = k2[dy, dx].astype(F32)

    two[...] = jnp.zeros(two.shape, F32)
    put(two, 0, 0, (0, 1, 2))
    w2first[...] = two[0:72, :].astype(BF16)
    two[...] = jnp.zeros(two.shape, F32)
    put(two, 0, 0, (1, 2))
    put(two, 72, 2 * HID, (2,))
    w2rest[...] = two[...].astype(BF16)
    two[...] = jnp.zeros(two.shape, F32)
    put(two, 0, 0, (0,))
    put(two, 72, HID, (0, 1))
    w2own[...] = two[...].astype(BF16)

    def lay(row, col, lags):
        for i, lag in enumerate(lags):
            for dy in range(3):
                for dx in range(3):
                    at = row + 32 * dy + 8 * dx + 2 * lag
                    c = col + HID * i
                    sq[at : at + 2, c : c + HID] = k2[dy, dx].astype(F32)

    sq[...] = jnp.zeros(sq.shape, F32)
    lay(0, 0, (0, 1, 2))
    w2b[...] = sq[0:96, :].T.astype(BF16)
    sq[...] = jnp.zeros(sq.shape, F32)
    lay(0, 0, (1, 2))
    lay(96, 2 * HID, (2,))
    w2brest[...] = sq[...].T.astype(BF16)


def weights(k1, k2):
    return call(
        weights_kernel,
        [
            ((HID, 9 * CH), BF16),
            ((HID, 9 * CH), BF16),
            ((2 * HID, 9 * CH), BF16),
            ((144, 192), BF16),
            ((72, 192), BF16),
            ((144, 192), BF16),
            ((192, 96), BF16),
            ((192, 192), BF16),
            ((3 * CH, 3 * HID), BF16),
            ((3 * CH, 3 * HID), BF16),
            ((3 * CH, 6 * HID), BF16),
        ],
        [
            ((2 * HID, 9 * CH), F32),
            ((6 * CH, 3 * HID), F32),
            ((3 * CH, 6 * HID), F32),
            ((144, 192), F32),
            ((192, 192), F32),
        ],
        4,
        "weights",
        0,
        k1,
        k2,
    )


def spread_row(x, xd, j, r):
    xd[j, r, 0:CH, :] = from_left(x).astype(BF16)
    xd[j, r, CH : 2 * CH, :] = x.astype(BF16)
    xd[j, r, 2 * CH :, :] = from_right(x).astype(BF16)


def spread(feat, above, below, keep, has, xd, wide):
    for s in range(OWN):
        x = feat[s].astype(F32)
        wide[s] = x if keep is None else x * keep
    scale = has if keep is None else [keep * h for h in has]
    for s in range(OWN):
        for r in range(TR):
            spread_row(wide[s, :, r, :], xd, s, HALO + r)
        for r in range(HALO):
            at = (r * OWN + s) * CH
            spread_row(above[at : at + CH, :].astype(F32) * scale[0], xd, s, r)
            spread_row(below[at : at + CH, :].astype(F32) * scale[1], xd, s, HALO + TR + r)


def taps(rows, pick):
    return jnp.concatenate(
        [jnp.concatenate([pick(r), pick(r + 1)], axis=1) for r in rows], axis=0
    )


def halves(ref, r, first, x):
    n = x.shape[0]
    ref[r, first : first + n, :] = x[:, :COLS]
    ref[r + 1, first : first + n, :] = x[:, COLS:]


def pair_row(ref, r, first, n):
    return jnp.concatenate(
        [ref[r, first : first + n, :], ref[r + 1, first : first + n, :]], axis=1
    )


def gather_columns(p):
    return from_right(p[:CH]) + p[CH : 2 * CH] + from_left(p[2 * CH :])


def own_kernel(
    valid, feat, above, below, vgrad, wcur, wboth, bias, w2own,
    cur, hown, town, cot,
    wide, xd,
):
    row0 = first_row()
    has = has_tiles()
    ends = [
        (above[EDGE:, :].astype(F32) * has[0], 0),
        (below[EDGE:, :].astype(F32) * has[1], TR + 2),
    ]
    for s in range(OWN):
        for c in range(2):
            at = s * 4 + c * 2
            for ext, first in ends:
                cot[s, c, first : first + 2, :] = ext[at : at + 2] + ext[12 + at : 14 + at]
            pos = row0 + lax.broadcasted_iota(jnp.int32, (TR, COLS), 0)
            cot[s, c, 2 : 2 + TR, :] = jnp.where(pos < valid[s], vgrad[s, c], 0.0)
    spread(feat, above, below, None, has, xd, wide)

    def step(i, carry):
        r = 2 * i
        rhs = [taps((r, r + 1, r + 2), lambda q, j=j: xd[j, q]) for j in range(OWN)]
        ear = []
        for j in range(2):
            both = dot(wboth[...], rhs[j])
            halves(cur, r, HID * j, both[:HID] + bias[...])
            ear.append(both[HID:])
            if j == 1:
                mid = both[:HID] + bias[...]
        last = dot(wcur[...], rhs[2]) + bias[...]
        halves(cur, r, 2 * HID, last)
        h = jnp.concatenate(
            [jnp.maximum(mid + ear[0], 0.0), jnp.maximum(last + ear[1], 0.0),
             jnp.maximum(last + ear[0], 0.0)],
            axis=0,
        ).astype(BF16)
        halves(hown, r, 0, h)
        halves(town, r, 0, dot(w2own[...], h))
        return carry

    lax.fori_loop(0, HID_ROWS // 2, step, 0, unroll=True)


def own(valid, *args):
    return call(
        own_kernel,
        [
            ((HID_ROWS, OWN * HID, COLS), F32),
            ((HID_ROWS, 3 * HID, COLS), BF16),
            ((HID_ROWS, 144, COLS), F32),
            ((OWN, 2, 24, COLS), F32),
        ],
        [((OWN, CH, TR, COLS), F32), ((OWN, FEAT_ROWS, 3 * CH, COLS), BF16)],
        8,
        "own",
        1,
        valid,
        *args,
    )


def fields_stage(hmid, town, w2first, w2rest, bias2, has, tsum, fld):
    def step(i, carry):
        r = 2 * i
        halves(tsum, r, 0, dot(w2first[...], pair_row(hmid, r, 0, 192)))
        rest = dot(w2rest[...], pair_row(hmid, r, 192, 192))
        halves(tsum, r, 72, rest + pair_row(town, r, 0, 144))
        return carry

    lax.fori_loop(0, HID_ROWS // 2, step, 0, unroll=True)
    for r in range(FLD_ROWS):
        for s in range(OWN):
            sums = []
            for dx in range(3):
                terms = []
                for dy in range(3):
                    at = 72 * s + 8 * (3 * dy + dx)
                    t = tsum[r + dy, at : at + 8, :]
                    if r + dy < 3:
                        t = t * has[0]
                    elif r + dy > HID_ROWS - 4:
                        t = t * has[1]
                    terms.append(t)
                sums.append(terms[0] + terms[1] + terms[2])
            fld[s, r] = (sums[1] + bias2[...]) + (from_left(sums[0]) + from_right(sums[2]))


def vote_stage(sharp, cot, fld, grd, g3, votes):
    for s in range(OWN):
        f = [[fld[s, :, 2 * k + c, :] for c in range(2)] for k in range(3)]
        beta = sharp[s]
        diff = {}
        dist = {}
        for a, b in ((0, 1), (0, 2), (1, 2)):
            diff[a, b] = [f[a][c] - f[b][c] for c in range(2)]
            dist[a, b] = diff[a, b][0] * diff[a, b][0] + diff[a, b][1] * diff[a, b][1]
        score = [dist[0, 1] + dist[0, 2], dist[0, 1] + dist[1, 2], dist[0, 2] + dist[1, 2]]
        logit = [-beta * q for q in score]
        top = jnp.maximum(jnp.maximum(logit[0], logit[1]), logit[2])
        expo = [jnp.exp(q - top) for q in logit]
        inv = 1.0 / (expo[0] + expo[1] + expo[2])
        w = [q * inv for q in expo]
        v = [w[0] * f[0][c] + w[1] * f[1][c] + w[2] * f[2][c] for c in range(2)]
        for c in range(2):
            votes[s, c, 0:FLD_ROWS, :] = v[c]
        g = [cot[s, c, 0:FLD_ROWS, :] for c in range(2)]
        e = [
            -beta * w[k] * (g[0] * (f[k][0] - v[0]) + g[1] * (f[k][1] - v[1])) for k in range(3)
        ]
        pair = {key: 2.0 * (e[key[0]] + e[key[1]]) for key in diff}
        for c in range(2):
            m01 = pair[0, 1] * diff[0, 1][c]
            m02 = pair[0, 2] * diff[0, 2][c]
            m12 = pair[1, 2] * diff[1, 2][c]
            grd[s, :, 0 + c, :] = w[0] * g[c] + m01 + m02
            grd[s, :, 2 + c, :] = w[1] * g[c] - m01 + m12
            grd[s, :, 4 + c, :] = w[2] * g[c] - m02 - m12
        grd[s, :, 6, :] = jnp.zeros((FLD_ROWS, COLS), F32)
        grd[s, :, 7, :] = jnp.zeros((FLD_ROWS, COLS), F32)
    for r in range(FLD_ROWS):
        for s in range(OWN):
            x = grd[s, r]
            g3[s, r] = jnp.concatenate(
                [from_right(x), x, from_left(x), jnp.zeros_like(x)], axis=0
            ).astype(BF16)


def inside(ref, has):
    for r, h in ((0, has[0]), (DH_ROWS - 1, has[1])):
        ref[r] = (ref[r].astype(F32) * h).astype(BF16)


def low_grad_stage(w2b, w2brest, g3, hmid, has, dlow):
    def step(i, carry):
        q = 2 * i
        rhs = [taps((q + 2, q + 1, q), lambda r, s=s: g3[s, r]) for s in range(OWN)]
        h = [pair_row(hmid, q + 2, 192 * j, 192).astype(F32) for j in range(2)]
        first = jnp.where(h[0] > 0.0, dot(w2b[...], rhs[0]), 0.0)
        rest = jnp.where(
            h[1] > 0.0, dot(w2brest[...], jnp.concatenate([rhs[1], rhs[2]], axis=0)), 0.0
        )
        low = jnp.concatenate(
            [
                first[2 * HID :],
                first[HID : 2 * HID] + rest[HID : 2 * HID],
                first[:HID] + rest[:HID] + rest[2 * HID :],
            ],
            axis=0,
        ).astype(BF16)
        halves(dlow, q, 0, low)
        return carry

    lax.fori_loop(0, DH_ROWS // 2, step, 0, unroll=True)
    inside(dlow, has)


def feature_grad_stage(dref, jobs):
    def step(i, carry):
        r = 2 * i
        for first, size, weight, out, s in jobs:
            rhs = taps((r + 2, r + 1, r), lambda q: dref[q, first : first + size, :])
            p = dot(weight[...], rhs)
            for d in range(2):
                out[r + d, s] = gather_columns(p[:, COLS * d : COLS * d + COLS]).astype(out.dtype)
        return carry

    lax.fori_loop(0, TR // 2, step, 0, unroll=True)


def borrowed_kernel(
    sharp, prev, pabove, pbelow, cur, town, cot, wear, w2first, w2rest, bias2, w2b, w2brest, wgear,
    low, hmid, g3, votes,
    wide, xd, tsum, fld, grd, dlow,
):
    has = has_tiles()
    keep = (lax.axis_index("sec") > 0).astype(F32)
    spread(prev, pabove, pbelow, keep, has, xd, wide)

    def step(i, carry):
        r = 2 * i
        ear = [
            dot(wear[...], taps((r, r + 1, r + 2), lambda q, j=j: xd[j, q])) for j in range(OWN)
        ]
        c = pair_row(cur, r, 0, OWN * HID)
        c = [c[HID * s : HID * s + HID] for s in range(OWN)]
        h = jnp.concatenate(
            [
                jnp.maximum(c[s] + ear[3 + s - k], 0.0)
                for s, k in ((0, 1), (0, 2), (0, 3), (1, 2), (1, 3), (2, 3))
            ],
            axis=0,
        ).astype(BF16)
        halves(hmid, r, 0, h)
        return carry

    lax.fori_loop(0, HID_ROWS // 2, step, 0, unroll=True)
    fields_stage(hmid, town, w2first, w2rest, bias2, has, tsum, fld)
    vote_stage(sharp, cot, fld, grd, g3, votes)
    low_grad_stage(w2b, w2brest, g3, hmid, has, dlow)
    feature_grad_stage(dlow, [(64 * s, 64, wgear, low, s) for s in range(OWN)])


def borrowed(sharp, *args):
    return call(
        borrowed_kernel,
        [
            ((TR, OWN, CH, COLS), BF16),
            ((HID_ROWS, 6 * HID, COLS), BF16),
            ((OWN, FLD_ROWS, 32, COLS), BF16),
            ((OWN, 2, 24, COLS), F32),
        ],
        [
            ((OWN, CH, TR, COLS), F32),
            ((OWN, FEAT_ROWS, 3 * CH, COLS), BF16),
            ((HID_ROWS, OWN * 72, COLS), F32),
            ((OWN, FLD_ROWS, 8, COLS), F32),
            ((OWN, FLD_ROWS, 8, COLS), F32),
            ((DH_ROWS, 3 * HID, COLS), BF16),
        ],
        12,
        "borrowed",
        1,
        sharp,
        *args,
    )


def own_grad_kernel(votes, g3, hown, hmid, w2b, wgcur, wgboth, voted, grad, down):
    has = has_tiles()
    for s in range(OWN):
        for c in range(2):
            voted[s, c] = votes[s, c, 2 : 2 + TR, :]

    def step(i, carry):
        q = 2 * i
        ho = pair_row(hown, q + 2, 0, 192)
        hm = pair_row(hmid, q + 2, 0, 384)
        h = [
            hm[:192],
            jnp.concatenate([ho[:64], hm[192:320]], axis=0),
            jnp.concatenate([ho[64:], hm[320:]], axis=0),
        ]
        m = []
        for s in range(OWN):
            dh = dot(w2b[...], taps((q + 2, q + 1, q), lambda r, s=s: g3[s, r]))
            dh = jnp.where(h[s].astype(F32) > 0.0, dh, 0.0)
            m.append([dh[HID * k : HID * k + HID] for k in range(3)])
        c = [m[s][0] + m[s][1] + m[s][2] for s in range(OWN)]
        d = jnp.concatenate([c[0], m[1][0] + m[2][1], c[1], m[2][0], c[2]], axis=0).astype(BF16)
        halves(down, q, 0, d)
        return carry

    lax.fori_loop(0, DH_ROWS // 2, step, 0, unroll=3)
    inside(down, has)
    feature_grad_stage(
        down, [(0, 128, wgboth, grad, 0), (128, 128, wgboth, grad, 1), (256, 64, wgcur, grad, 2)]
    )


def own_grad(*args):
    return call(
        own_grad_kernel,
        [((OWN, 2, TR, COLS), F32), ((TR, OWN, CH, COLS), F32)],
        [((DH_ROWS, 5 * HID, COLS), BF16)],
        6,
        "own_grad",
        0,
        *args,
    )


def finish_kernel(grad, back, out):
    keep = (lax.axis_index("sec") < lax.axis_size("sec") - 1).astype(F32)
    for s in range(OWN):
        for r in range(TR):
            out[s, :, r, :] = grad[r, s] + back[r, s].astype(F32) * keep


def finish(grad, back):
    return call(finish_kernel, [((OWN, CH, TR, COLS), F32)], [], 4, "finish", 0, grad, back)[0]


def shift(value, secs, tiles):
    n, m = lax.axis_size("sec"), lax.axis_size("tile")
    pairs = [
        (a * m + b, ((a + secs) % n) * m + (b + tiles) % m) for a in range(n) for b in range(m)
    ]
    return lax.ppermute(value, ("sec", "tile"), pairs)


def body(
    features, vote_grad, sharpness, valid_rows, first_kernel, first_bias, second_kernel, second_bias
):
    prev = shift(features, 1, 0)
    top, bottom = edges(valid_rows, features, vote_grad)
    above = shift(bottom, 0, 1)
    below = shift(top, 0, -1)
    pabove = shift(bottom, 1, 1)
    pbelow = shift(top, 1, -1)
    (
        wcur, wear, wboth, w2own, w2first, w2rest, w2b, w2brest, wgear, wgcur, wgboth,
    ) = weights(first_kernel, second_kernel)
    bias = first_bias[:, None]
    bias2 = jnp.tile(second_bias, 4)[:, None]
    cur, hown, town, cot = own(
        valid_rows, features, above, below, vote_grad, wcur, wboth, bias, w2own
    )
    low, hmid, g3, votes = borrowed(
        sharpness, prev, pabove, pbelow, cur, town, cot,
        wear, w2first, w2rest, bias2, w2b, w2brest, wgear,
    )
    back = shift(low, -1, 0)
    voted, grad = own_grad(votes, g3, hown, hmid, w2b, wgcur, wgboth)
    return (voted, finish(grad, back))


def solution(mesh):
    return jax.shard_map(
        body,
        mesh=mesh,
        in_specs=(
            P("sec", None, "tile", None),
            P("sec", None, "tile", None),
            P("sec"),
            P("sec"),
            P(),
            P(),
            P(),
            P(),
        ),
        out_specs=(P("sec", None, "tile", None), P("sec", None, "tile", None)),
        check_vma=False,
    )
```

```python
import jax
import jax.numpy as jnp
from jax import lax
from jax.experimental import pallas as pl
from jax.experimental.pallas import tpu as pltpu
from jax.sharding import PartitionSpec as P

F32 = jnp.float32
BF16 = jnp.bfloat16
OWN = 3
CH = 32
HID = 64
TR = 16
COLS = 128
HALO = 4
FEAT_ROWS = TR + 2 * HALO
HID_ROWS = FEAT_ROWS - 2
FLD_ROWS = FEAT_ROWS - 4
DH_ROWS = FEAT_ROWS - 6
EDGE = HALO * OWN * CH
EDGE_ALL = EDGE + 32


def lane(shape):
    return lax.broadcasted_iota(jnp.int32, shape, len(shape) - 1)


def from_left(x):
    return jnp.where(lane(x.shape) == 0, 0.0, pltpu.roll(x, 1, x.ndim - 1))


def from_right(x):
    return jnp.where(lane(x.shape) == COLS - 1, 0.0, pltpu.roll(x, COLS - 1, x.ndim - 1))


def dot(a, b):
    return jnp.dot(a, b, preferred_element_type=F32)


def params(mib):
    return pltpu.CompilerParams(vmem_limit_bytes=mib << 20)


COST = {
    "own_rim": 0,
    "edges": 0,
    "weights": 0,
    "own_inner": 0,
    "middle": 2306,
    "borrowed": 3459,
    "own_grad": 3459,
    "finish": 1153,
}
INNER = TR - 2
RIM = HID_ROWS - INNER
INNER_PAIRS = [HALO + 2 * i for i in range(INNER // 2)]
RIM_PAIRS = [0, 2, HALO + INNER, HALO + INNER + 2]


def call(kernel, outs, scratch, mib, name, specs, *args):
    space = {"v": pltpu.VMEM, "h": pltpu.HBM}
    args = [
        pltpu.with_memory_space_constraint(x, pltpu.HBM) if c == "h" else x
        for x, c in zip(args, specs, strict=True)
    ]
    return pl.pallas_call(
        kernel,
        out_shape=tuple(jax.ShapeDtypeStruct(shape, kind) for shape, kind in outs),
        in_specs=[pl.BlockSpec(memory_space=space[c]) for c in specs],
        out_specs=(pl.BlockSpec(memory_space=pltpu.VMEM),) * len(outs),
        scratch_shapes=[
            item[0](item[1], item[2]) if len(item) == 3 else pltpu.VMEM(*item) for item in scratch
        ],
        compiler_params=params(mib),
        cost_estimate=pl.CostEstimate(
            flops=COST[name] * 10**6, bytes_accessed=0, transcendentals=0
        ),
        name=name,
    )(*args)


def sems(shape, _):
    return pltpu.SemaphoreType.DMA(shape)


def fetch(sems, *moves):
    copies = [pltpu.make_async_copy(a, b, sems.at[i]) for i, (a, b) in enumerate(moves)]
    for c in copies:
        c.start()
    for c in copies:
        c.wait()


def odd_tile():
    return lax.axis_index("tile") % 2 == 1


def has_tiles():
    tile = lax.axis_index("tile")
    return (tile > 0).astype(F32), (tile < lax.axis_size("tile") - 1).astype(F32)


class Rows:
    def __init__(self, inner, rim):
        self.inner, self.rim = inner, rim

    def at(self, r):
        if r < HALO:
            return self.rim, r
        if r < HALO + INNER:
            return self.inner, r - HALO
        return self.rim, r - INNER

    def pair(self, r, first, n):
        ref, i = self.at(r)
        return pair_row(ref, i, first, n)

    def put(self, r, first, x):
        ref, i = self.at(r)
        halves(ref, i, first, x)


def edges_kernel(
    valid_hbm, sharp_hbm, b2_hbm, feat_hbm, vgrad_hbm,
    sibling, outer, wide, cot, consts,
    valid, sharp, b2, feat, vgrad, ext, sems,
):
    fetch(
        sems,
        (feat_hbm, feat), (vgrad_hbm, vgrad), (valid_hbm, valid), (sharp_hbm, sharp), (b2_hbm, b2),
    )
    row0 = lax.axis_index("tile") * TR
    odd = odd_tile()
    for s in range(OWN):
        wide[s] = feat[s].astype(F32)
        pos = row0 + lax.broadcasted_iota(jnp.int32, (TR, COLS), 0)
        for c in range(2):
            cot[s, c] = jnp.where(pos < valid[s], vgrad[s, c], 0.0)
        consts[s] = jnp.full((8, COLS), sharp[s], F32)
    even_row = lax.broadcasted_iota(jnp.int32, (8, COLS), 0) % 2 == 0
    consts[OWN] = jnp.where(even_row, b2[0], b2[1])
    for out, last in ((sibling, jnp.logical_not(odd)), (outer, odd)):
        ext[...] = jnp.zeros((32, COLS), F32)
        for s in range(OWN):
            for c in range(2):
                x = jnp.where(last, cot[s, c, TR - 2 :, :], cot[s, c, 0:2, :])
                high = x.astype(BF16).astype(F32)
                at = s * 4 + c * 2
                ext[at : at + 2, :] = high
                ext[12 + at : 14 + at, :] = x - high
        out[EDGE:, :] = ext[...].astype(BF16)
        for s in range(OWN):
            for r in range(HALO):
                at = (r * OWN + s) * CH
                x = jnp.where(last, wide[s, :, TR - HALO + r, :], wide[s, :, r, :])
                out[at : at + CH, :] = x.astype(BF16)


def edges(*args):
    return call(
        edges_kernel,
        [
            ((EDGE_ALL, COLS), BF16),
            ((EDGE_ALL, COLS), BF16),
            ((OWN, CH, TR, COLS), F32),
            ((OWN, 2, TR, COLS), F32),
            ((OWN + 1, 8, COLS), F32),
        ],
        [
            (pltpu.SMEM, (OWN,), jnp.int32),
            (pltpu.SMEM, (OWN,), F32),
            (pltpu.SMEM, (2,), F32),
            ((OWN, CH, TR, COLS), BF16),
            ((OWN, 2, TR, COLS), F32),
            ((32, COLS), F32),
            (sems, (5,), None),
        ],
        3,
        "edges",
        "hhhhh",
        *args,
    )


def weights_kernel(
    k1_hbm, k2_hbm, b1_hbm, wcur, wear, wboth, w2own, w2first, w2rest, w2b, w2brest, wgear, wgcur, wgboth, bias,
    k1, k2, b1, fwd, bwd, both, two, sq, sems,
):
    fetch(sems, (k1_hbm, k1), (k2_hbm, k2), (b1_hbm, b1))
    bias[...] = jnp.broadcast_to(b1[...], (COLS, HID)).T
    for dy in range(3):
        for dx in range(3):
            k = k1[dy, dx].astype(F32)
            t = CH * (3 * dy + dx)
            fwd[0:HID, t : t + CH] = k[:, :CH]
            fwd[HID:, t : t + CH] = k[:, CH:]
            kt = k.T
            rows = slice(CH * dx, CH * dx + CH)
            bwd[rows, HID * dy : HID * dy + HID] = kt[:CH]
            bwd[3 * CH + CH * dx : 4 * CH + CH * dx, HID * dy : HID * dy + HID] = kt[CH:]
            both[rows, 2 * HID * dy : 2 * HID * dy + HID] = kt[:CH]
            both[rows, 2 * HID * dy + HID : 2 * HID * dy + 2 * HID] = kt[CH:]
    wcur[...] = fwd[0:HID, :].astype(BF16)
    wear[...] = fwd[HID:, :].astype(BF16)
    wboth[...] = fwd[...].astype(BF16)
    wgcur[...] = bwd[0 : 3 * CH, :].astype(BF16)
    wgear[...] = bwd[3 * CH :, :].astype(BF16)
    wgboth[...] = both[...].astype(BF16)

    def put(ref, row, col, lags):
        for i, lag in enumerate(lags):
            for dy in range(3):
                for dx in range(3):
                    at = row + 8 * (3 * dy + dx) + 2 * lag
                    c = col + HID * i
                    ref[at : at + 2, c : c + HID] = k2[dy, dx].astype(F32)

    two[...] = jnp.zeros(two.shape, F32)
    put(two, 0, 0, (0, 1, 2))
    w2first[...] = two[0:72, :].astype(BF16)
    two[...] = jnp.zeros(two.shape, F32)
    put(two, 0, 0, (1, 2))
    put(two, 72, 2 * HID, (2,))
    w2rest[...] = two[...].astype(BF16)
    two[...] = jnp.zeros(two.shape, F32)
    put(two, 0, 0, (0,))
    put(two, 72, HID, (0, 1))
    w2own[...] = two[...].astype(BF16)

    def lay(row, col, lags):
        for i, lag in enumerate(lags):
            for dy in range(3):
                for dx in range(3):
                    at = row + 32 * dy + 8 * dx + 2 * lag
                    c = col + HID * i
                    sq[at : at + 2, c : c + HID] = k2[dy, dx].astype(F32)

    sq[...] = jnp.zeros(sq.shape, F32)
    lay(0, 0, (0, 1, 2))
    w2b[...] = sq[0:96, :].T.astype(BF16)
    sq[...] = jnp.zeros(sq.shape, F32)
    lay(0, 0, (1, 2))
    lay(96, 2 * HID, (2,))
    w2brest[...] = sq[...].T.astype(BF16)


def weights(k1, k2, b1):
    return call(
        weights_kernel,
        [
            ((HID, 9 * CH), BF16),
            ((HID, 9 * CH), BF16),
            ((2 * HID, 9 * CH), BF16),
            ((144, 192), BF16),
            ((72, 192), BF16),
            ((144, 192), BF16),
            ((192, 96), BF16),
            ((192, 192), BF16),
            ((3 * CH, 3 * HID), BF16),
            ((3 * CH, 3 * HID), BF16),
            ((3 * CH, 6 * HID), BF16),
            ((HID, COLS), F32),
        ],
        [
            (k1.shape, BF16),
            (k2.shape, BF16),
            (b1.shape, F32),
            ((2 * HID, 9 * CH), F32),
            ((6 * CH, 3 * HID), F32),
            ((3 * CH, 6 * HID), F32),
            ((144, 192), F32),
            ((192, 192), F32),
            (sems, (3,), None),
        ],
        4,
        "weights",
        "hhh",
        k1,
        k2,
        b1,
    )


def spread_row(x, xd, j, r):
    xd[j, r, 0:CH, :] = from_left(x).astype(BF16)
    xd[j, r, CH : 2 * CH, :] = x.astype(BF16)
    xd[j, r, 2 * CH :, :] = from_right(x).astype(BF16)


def spread_own(wide, keep, xd):
    for s in range(OWN):
        for r in range(TR):
            x = wide[s, :, r, :]
            spread_row(x if keep is None else x * keep, xd, s, r)


def spread_rim(pick, scale, xr):
    for s in range(OWN):
        for r in range(HALO):
            for side in range(2):
                spread_row(pick(side, s, r) * scale[side], xr, s, HALO * side + r)


def feature_rows(xd, xr):
    def pick(j, r):
        if r < HALO:
            return xr[j, r]
        if r < HALO + TR:
            return xd[j, r - HALO]
        return xr[j, r - TR]

    return pick


def taps(rows, pick):
    return jnp.concatenate(
        [jnp.concatenate([pick(r), pick(r + 1)], axis=1) for r in rows], axis=0
    )


def halves(ref, r, first, x):
    n = x.shape[0]
    ref[r, first : first + n, :] = x[:, :COLS]
    ref[r + 1, first : first + n, :] = x[:, COLS:]


def pair_row(ref, r, first, n):
    return jnp.concatenate(
        [ref[r, first : first + n, :], ref[r + 1, first : first + n, :]], axis=1
    )


def gather_columns(p):
    return from_right(p[:CH]) + p[CH : 2 * CH] + from_left(p[2 * CH :])


def hidden_own(pairs, pick, wcur, wboth, bias, w2own, cur, hown, town):
    b = jnp.concatenate([bias[...], bias[...]], axis=1)
    for r in pairs:
        rhs = [taps((r, r + 1, r + 2), lambda q, j=j: pick(j, q)) for j in range(OWN)]
        both = [dot(wboth[...], rhs[j]) for j in range(2)]
        c = [both[0][:HID] + b, both[1][:HID] + b, dot(wcur[...], rhs[2]) + b]
        ear = [both[0][HID:], both[1][HID:]]
        for s in range(OWN):
            cur.put(r, HID * s, c[s])
        h = jnp.concatenate(
            [jnp.maximum(x, 0.0) for x in (c[1] + ear[0], c[2] + ear[1], c[2] + ear[0])], axis=0
        ).astype(BF16)
        hown.put(r, 0, h)
        town.put(r, 0, dot(w2own[...], h))


def hidden_borrowed(pairs, pick, wear, w2first, w2rest, cur, town, hmid, tsum):
    for r in pairs:
        ear = [
            dot(wear[...], taps((r, r + 1, r + 2), lambda q, j=j: pick(j, q)))
            for j in range(OWN)
        ]
        c = [cur.pair(r, HID * s, HID) for s in range(OWN)]
        h = [
            jnp.concatenate([jnp.maximum(c[s] + ear[3 + s - k], 0.0) for s, k in part], axis=0)
            for part in (((0, 1), (0, 2), (0, 3)), ((1, 2), (1, 3), (2, 3)))
        ]
        h = [x.astype(BF16) for x in h]
        hmid.put(r, 0, h[0])
        hmid.put(r, 192, h[1])
        tsum.put(r, 0, dot(w2first[...], h[0]))
        tsum.put(r, 72, dot(w2rest[...], h[1]) + town.pair(r, 0, 144))


def own_kernel(wide, wcur, wboth, bias, w2own, xd, cur, hown, town):
    spread_own(wide, None, xd)
    hidden_own(
        INNER_PAIRS, feature_rows(xd, None), wcur, wboth, bias, w2own,
        Rows(cur, None), Rows(hown, None), Rows(town, None),
    )


def hidden_outs(n):
    return [
        ((n, OWN * HID, COLS), F32),
        ((n, 3 * HID, COLS), BF16),
        ((n, 144, COLS), F32),
    ]


def own_inner(*args):
    return call(
        own_kernel,
        [((OWN, TR, 3 * CH, COLS), BF16)] + hidden_outs(INNER),
        [],
        2,
        "own_inner",
        "v" * len(args),
        *args,
    )


def rim_kernel(
    sibling, outer, cot16, xd, wcur, wboth, bias, w2own, rcur, rhown, rtown, cot, xr
):
    odd = odd_tile()
    has = has_tiles()

    def halo(side, first, n):
        x, y = sibling[first : first + n, :], outer[first : first + n, :]
        x, y = x.astype(F32), y.astype(F32)
        return jnp.where(odd, x, y) if side == 0 else jnp.where(odd, y, x)

    for side, first in ((0, 0), (1, TR + 2)):
        ext = halo(side, EDGE, 32) * has[side]
        for s in range(OWN):
            for c in range(2):
                at = s * 4 + c * 2
                cot[s, c, first : first + 2, :] = ext[at : at + 2] + ext[12 + at : 14 + at]
    for s in range(OWN):
        for c in range(2):
            cot[s, c, 2 : 2 + TR, :] = cot16[s, c]
    spread_rim(lambda side, s, r: halo(side, (r * OWN + s) * CH, CH), has, xr)
    hidden_own(
        RIM_PAIRS, feature_rows(xd, xr), wcur, wboth, bias, w2own,
        Rows(None, rcur), Rows(None, rhown), Rows(None, rtown),
    )


def own_rim(*args):
    return call(
        rim_kernel,
        hidden_outs(RIM) + [((OWN, 2, 24, COLS), F32)],
        [((OWN, 2 * HALO, 3 * CH, COLS), BF16)],
        2,
        "own_rim",
        "v" * len(args),
        *args,
    )


def middle_kernel(prev, icur, itown, wear, w2first, w2rest, xp, ihmid, itsum, wide):
    keep = (lax.axis_index("sec") > 0).astype(F32)
    for s in range(OWN):
        wide[s] = prev[s].astype(F32)
    spread_own(wide, keep, xp)
    hidden_borrowed(
        INNER_PAIRS, feature_rows(xp, None), wear, w2first, w2rest,
        Rows(icur, None), Rows(itown, None), Rows(ihmid, None), Rows(itsum, None),
    )


def middle(*args):
    return call(
        middle_kernel,
        [
            ((OWN, TR, 3 * CH, COLS), BF16),
            ((INNER, 6 * HID, COLS), BF16),
            ((INNER, OWN * 72, COLS), F32),
        ],
        [((OWN, CH, TR, COLS), F32)],
        3,
        "middle",
        "v" * len(args),
        *args,
    )


def fields_stage(tsum, bias2, has, fld):
    for r in range(FLD_ROWS):
        for s in range(OWN):
            sums = []
            for dx in range(3):
                terms = []
                for dy in range(3):
                    at = 72 * s + 8 * (3 * dy + dx)
                    ref, i = tsum.at(r + dy)
                    t = ref[i, at : at + 8, :]
                    if r + dy < 3:
                        t = t * has[0]
                    elif r + dy > HID_ROWS - 4:
                        t = t * has[1]
                    terms.append(t)
                sums.append(terms[0] + terms[1] + terms[2])
            fld[s, r] = (sums[1] + bias2[...]) + (from_left(sums[0]) + from_right(sums[2]))


def vote_stage(consts, cot, fld, grd, g3, votes):
    for s in range(OWN):
        f = [[fld[s, :, 2 * k + c, :] for c in range(2)] for k in range(3)]
        beta = consts[s, 0:1, :]
        diff = {}
        dist = {}
        for a, b in ((0, 1), (0, 2), (1, 2)):
            diff[a, b] = [f[a][c] - f[b][c] for c in range(2)]
            dist[a, b] = diff[a, b][0] * diff[a, b][0] + diff[a, b][1] * diff[a, b][1]
        score = [dist[0, 1] + dist[0, 2], dist[0, 1] + dist[1, 2], dist[0, 2] + dist[1, 2]]
        logit = [-beta * q for q in score]
        top = jnp.maximum(jnp.maximum(logit[0], logit[1]), logit[2])
        expo = [jnp.exp(q - top) for q in logit]
        inv = 1.0 / (expo[0] + expo[1] + expo[2])
        w = [q * inv for q in expo]
        v = [w[0] * f[0][c] + w[1] * f[1][c] + w[2] * f[2][c] for c in range(2)]
        for c in range(2):
            votes[s, c, 0:FLD_ROWS, :] = v[c]
        g = [cot[s, c, 0:FLD_ROWS, :] for c in range(2)]
        e = [
            -beta * w[k] * (g[0] * (f[k][0] - v[0]) + g[1] * (f[k][1] - v[1])) for k in range(3)
        ]
        pair = {key: 2.0 * (e[key[0]] + e[key[1]]) for key in diff}
        for c in range(2):
            m01 = pair[0, 1] * diff[0, 1][c]
            m02 = pair[0, 2] * diff[0, 2][c]
            m12 = pair[1, 2] * diff[1, 2][c]
            grd[s, :, 0 + c, :] = w[0] * g[c] + m01 + m02
            grd[s, :, 2 + c, :] = w[1] * g[c] - m01 + m12
            grd[s, :, 4 + c, :] = w[2] * g[c] - m02 - m12
        grd[s, :, 6, :] = jnp.zeros((FLD_ROWS, COLS), F32)
        grd[s, :, 7, :] = jnp.zeros((FLD_ROWS, COLS), F32)
    for r in range(FLD_ROWS):
        for s in range(OWN):
            x = grd[s, r]
            g3[s, r] = jnp.concatenate(
                [from_right(x), x, from_left(x), jnp.zeros_like(x)], axis=0
            ).astype(BF16)


def inside(ref, has):
    for r, h in ((0, has[0]), (DH_ROWS - 1, has[1])):
        ref[r] = (ref[r].astype(F32) * h).astype(BF16)


def low_grad_stage(w2b, w2brest, g3, hmid, has, dlow):
    for q in range(0, DH_ROWS, 2):
        rhs = [taps((q + 2, q + 1, q), lambda r, s=s: g3[s, r]) for s in range(OWN)]
        h = [hmid.pair(q + 2, 192 * j, 192).astype(F32) for j in range(2)]
        first = jnp.where(h[0] > 0.0, dot(w2b[...], rhs[0]), 0.0)
        rest = jnp.where(
            h[1] > 0.0, dot(w2brest[...], jnp.concatenate([rhs[1], rhs[2]], axis=0)), 0.0
        )
        low = jnp.concatenate(
            [
                first[2 * HID :],
                first[HID : 2 * HID] + rest[HID : 2 * HID],
                first[:HID] + rest[:HID] + rest[2 * HID :],
            ],
            axis=0,
        ).astype(BF16)
        halves(dlow, q, 0, low)
    inside(dlow, has)


def feature_grad_stage(dref, jobs, unroll):
    def step(i, carry):
        r = 2 * i
        for first, size, weight, out, s in jobs:
            rhs = taps((r + 2, r + 1, r), lambda q: dref[q, first : first + size, :])
            p = dot(weight[...], rhs)
            for d in range(2):
                out[r + d, s] = gather_columns(p[:, COLS * d : COLS * d + COLS]).astype(out.dtype)
        return carry

    lax.fori_loop(0, TR // 2, step, 0, unroll=unroll)


def borrowed_kernel(
    psib, pouter, xp, rcur, rtown, itsum, ihmid, cot, consts,
    wear, w2first, w2rest, w2b, w2brest, wgear,
    low, rhmid, g3, votes,
    wide, xr, rtsum, fld, grd, dlow,
):
    odd = odd_tile()
    has = has_tiles()
    keep = (lax.axis_index("sec") > 0).astype(F32)
    for s in range(OWN):
        wide[s] = psib[s].astype(F32)

    def halo(side, s, r):
        at = (r * OWN + s) * CH
        y = pouter[at : at + CH, :].astype(F32)
        if side == 0:
            return jnp.where(odd, wide[s, :, TR - HALO + r, :], y)
        return jnp.where(odd, y, wide[s, :, r, :])

    spread_rim(halo, [keep * h for h in has], xr)
    hmid, tsum = Rows(ihmid, rhmid), Rows(itsum, rtsum)
    hidden_borrowed(
        RIM_PAIRS, feature_rows(xp, xr), wear, w2first, w2rest,
        Rows(None, rcur), Rows(None, rtown), hmid, tsum,
    )
    fields_stage(tsum, consts.at[OWN], has, fld)
    vote_stage(consts, cot, fld, grd, g3, votes)
    low_grad_stage(w2b, w2brest, g3, hmid, has, dlow)
    feature_grad_stage(dlow, [(64 * s, 64, wgear, low, s) for s in range(OWN)], True)


def borrowed(*args):
    return call(
        borrowed_kernel,
        [
            ((TR, OWN, CH, COLS), BF16),
            ((RIM, 6 * HID, COLS), BF16),
            ((OWN, FLD_ROWS, 32, COLS), BF16),
            ((OWN, 2, 24, COLS), F32),
        ],
        [
            ((OWN, CH, TR, COLS), F32),
            ((OWN, 2 * HALO, 3 * CH, COLS), BF16),
            ((RIM, OWN * 72, COLS), F32),
            ((OWN, FLD_ROWS, 8, COLS), F32),
            ((OWN, FLD_ROWS, 8, COLS), F32),
            ((DH_ROWS, 3 * HID, COLS), BF16),
        ],
        6,
        "borrowed",
        "v" * len(args),
        *args,
    )


def own_grad_kernel(
    votes, g3, ihown, rhown, ihmid, rhmid, w2b, wgcur, wgboth, voted, grad, down
):
    has = has_tiles()
    hown, hmid = Rows(ihown, rhown), Rows(ihmid, rhmid)
    for s in range(OWN):
        for c in range(2):
            voted[s, c] = votes[s, c, 2 : 2 + TR, :]
    for q in range(0, DH_ROWS, 2):
        ho = hown.pair(q + 2, 0, 192)
        hm = hmid.pair(q + 2, 0, 384)
        h = [
            hm[:192],
            jnp.concatenate([ho[:64], hm[192:320]], axis=0),
            jnp.concatenate([ho[64:], hm[320:]], axis=0),
        ]
        m = []
        for s in range(OWN):
            dh = dot(w2b[...], taps((q + 2, q + 1, q), lambda r, s=s: g3[s, r]))
            dh = jnp.where(h[s].astype(F32) > 0.0, dh, 0.0)
            m.append([dh[HID * k : HID * k + HID] for k in range(3)])
        c = [m[s][0] + m[s][1] + m[s][2] for s in range(OWN)]
        d = jnp.concatenate([c[0], m[1][0] + m[2][1], c[1], m[2][0], c[2]], axis=0).astype(BF16)
        halves(down, q, 0, d)
    inside(down, has)
    feature_grad_stage(
        down,
        [(0, 128, wgboth, grad, 0), (128, 128, wgboth, grad, 1), (256, 64, wgcur, grad, 2)],
        4,
    )


def own_grad(*args):
    return call(
        own_grad_kernel,
        [((OWN, 2, TR, COLS), F32), ((TR, OWN, CH, COLS), F32)],
        [((DH_ROWS, 5 * HID, COLS), BF16)],
        4,
        "own_grad",
        "v" * len(args),
        *args,
    )


def finish_kernel(grad, back, out):
    keep = (lax.axis_index("sec") < lax.axis_size("sec") - 1).astype(F32)
    for s in range(OWN):
        for r in range(TR):
            out[s, :, r, :] = grad[r, s] + back[r, s].astype(F32) * keep


def finish(grad, back):
    return call(finish_kernel, [((OWN, CH, TR, COLS), F32)], [], 4, "finish", "vv", grad, back)[0]


def move(value, secs, tile_to):
    n, m = lax.axis_size("sec"), lax.axis_size("tile")
    pairs = [(a * m + b, ((a + secs) % n) * m + tile_to(b)) for a in range(n) for b in range(m)]
    return lax.ppermute(value, ("sec", "tile"), pairs)


def body(
    features, vote_grad, sharpness, valid_rows, first_kernel, first_bias, second_kernel, second_bias
):
    tiles = lax.axis_size("tile")

    def same(b):
        return b

    def to_sibling(b):
        return b + 1 - 2 * (b % 2)

    def to_outer(b):
        return (b - 1 + 2 * (b % 2)) % tiles

    prev = move(features, 1, same)
    for_sibling, for_outer, wide, cot16, consts = edges(
        valid_rows, sharpness, second_bias, features, vote_grad
    )
    sibling = move(for_sibling, 0, to_sibling)
    outer = move(for_outer, 0, to_outer)
    pouter = move(for_outer, 1, to_outer)
    (
        wcur, wear, wboth, w2own, w2first, w2rest, w2b, w2brest, wgear, wgcur, wgboth, bias,
    ) = weights(first_kernel, second_kernel, first_bias[None])
    xd, icur, ihown, itown = own_inner(wide, wcur, wboth, bias, w2own)
    rcur, rhown, rtown, cot = own_rim(
        sibling, outer, cot16, xd, wcur, wboth, bias, w2own
    )
    prev, rcur, pouter = lax.optimization_barrier((prev, rcur, pouter))
    psib = move(prev, 0, to_sibling)
    xp, ihmid, itsum = middle(prev, icur, itown, wear, w2first, w2rest)
    low, rhmid, g3, votes = borrowed(
        psib, pouter, xp, rcur, rtown, itsum, ihmid, cot, consts,
        wear, w2first, w2rest, w2b, w2brest, wgear,
    )
    back = move(low, -1, same)
    voted, grad = own_grad(votes, g3, ihown, rhown, ihmid, rhmid, w2b, wgcur, wgboth)
    return (voted, finish(grad, back))


def solution(mesh):
    return jax.shard_map(
        body,
        mesh=mesh,
        in_specs=(
            P("sec", None, "tile", None),
            P("sec", None, "tile", None),
            P("sec"),
            P("sec"),
            P(),
            P(),
            P(),
            P(),
        ),
        out_specs=(P("sec", None, "tile", None), P("sec", None, "tile", None)),
        check_vma=False,
    )
```

```python
import jax
import jax.numpy as jnp
from jax import lax
from jax.experimental import pallas as pl
from jax.experimental.pallas import tpu as pltpu
from jax.sharding import PartitionSpec as P

F32 = jnp.float32
BF16 = jnp.bfloat16
OWN = 3
CH = 32
HID = 64
TR = 16
COLS = 128
HALO = 4
FEAT_ROWS = TR + 2 * HALO
HID_ROWS = FEAT_ROWS - 2
FLD_ROWS = FEAT_ROWS - 4
DH_ROWS = FEAT_ROWS - 6
EDGE = HALO * OWN * CH
EDGE_ALL = EDGE + 32


def lane(shape):
    return lax.broadcasted_iota(jnp.int32, shape, len(shape) - 1)


def from_left(x):
    return jnp.where(lane(x.shape) == 0, 0.0, pltpu.roll(x, 1, x.ndim - 1))


def from_right(x):
    return jnp.where(lane(x.shape) == COLS - 1, 0.0, pltpu.roll(x, COLS - 1, x.ndim - 1))


def dot(a, b):
    return jnp.dot(a, b, preferred_element_type=F32)


def params(mib):
    return pltpu.CompilerParams(vmem_limit_bytes=mib << 20)


COST = {
    "own_rim": 0,
    "edges": 0,
    "weights": 0,
    "own_inner": 0,
    "middle": 2306,
    "borrowed": 3459,
    "own_grad": 3459,
    "finish": 1153,
}
INNER = TR - 2
RIM = HID_ROWS - INNER
INNER_PAIRS = [HALO + 2 * i for i in range(INNER // 2)]
RIM_PAIRS = [0, 2, HALO + INNER, HALO + INNER + 2]
FLD_INNER = FLD_ROWS - 2 * HALO
DH_INNER = DH_ROWS - 2 * HALO
OUT_INNER = TR - 2 * HALO


def inner_rows(count, step=1):
    return range(HALO, HALO + count, step)


def rim_rows(count, step=1):
    return [*range(0, HALO, step), *range(HALO + count, 2 * HALO + count, step)]


def call(kernel, outs, scratch, mib, name, specs, *args):
    space = {"v": pltpu.VMEM, "h": pltpu.HBM}
    args = [
        pltpu.with_memory_space_constraint(x, pltpu.HBM) if c == "h" else x
        for x, c in zip(args, specs, strict=True)
    ]
    return pl.pallas_call(
        kernel,
        out_shape=tuple(jax.ShapeDtypeStruct(shape, kind) for shape, kind in outs),
        in_specs=[pl.BlockSpec(memory_space=space[c]) for c in specs],
        out_specs=(pl.BlockSpec(memory_space=pltpu.VMEM),) * len(outs),
        scratch_shapes=[
            item[0](item[1], item[2]) if len(item) == 3 else pltpu.VMEM(*item) for item in scratch
        ],
        compiler_params=params(mib),
        cost_estimate=pl.CostEstimate(
            flops=COST[name] * 10**6, bytes_accessed=0, transcendentals=0
        ),
        name=name,
    )(*args)


def sems(shape, _):
    return pltpu.SemaphoreType.DMA(shape)


def fetch(sems, *moves):
    copies = [pltpu.make_async_copy(a, b, sems.at[i]) for i, (a, b) in enumerate(moves)]
    for c in copies:
        c.start()
    for c in copies:
        c.wait()


def odd_tile():
    return lax.axis_index("tile") % 2 == 1


def has_tiles():
    tile = lax.axis_index("tile")
    return (tile > 0).astype(F32), (tile < lax.axis_size("tile") - 1).astype(F32)


class Rows:
    def __init__(self, inner, rim, count=INNER):
        self.inner, self.rim, self.count = inner, rim, count

    def at(self, r):
        if r < HALO:
            return self.rim, r
        if r < HALO + self.count:
            return self.inner, r - HALO
        return self.rim, r - self.count

    def pair(self, r, first, n):
        ref, i = self.at(r)
        return pair_row(ref, i, first, n)

    def put(self, r, first, x):
        ref, i = self.at(r)
        halves(ref, i, first, x)


def edges_kernel(
    valid_hbm, sharp_hbm, b2_hbm, feat_hbm, vgrad_hbm,
    sibling, outer, wide, cot, consts,
    valid, sharp, b2, feat, vgrad, ext, sems,
):
    fetch(
        sems,
        (feat_hbm, feat), (vgrad_hbm, vgrad), (valid_hbm, valid), (sharp_hbm, sharp), (b2_hbm, b2),
    )
    row0 = lax.axis_index("tile") * TR
    odd = odd_tile()
    for s in range(OWN):
        wide[s] = feat[s].astype(F32)
        pos = row0 + lax.broadcasted_iota(jnp.int32, (TR, COLS), 0)
        for c in range(2):
            cot[s, c] = jnp.where(pos < valid[s], vgrad[s, c], 0.0)
        consts[s] = jnp.full((8, COLS), sharp[s], F32)
    even_row = lax.broadcasted_iota(jnp.int32, (8, COLS), 0) % 2 == 0
    consts[OWN] = jnp.where(even_row, b2[0], b2[1])
    for out, last in ((sibling, jnp.logical_not(odd)), (outer, odd)):
        ext[...] = jnp.zeros((32, COLS), F32)
        for s in range(OWN):
            for c in range(2):
                x = jnp.where(last, cot[s, c, TR - 2 :, :], cot[s, c, 0:2, :])
                high = x.astype(BF16).astype(F32)
                at = s * 4 + c * 2
                ext[at : at + 2, :] = high
                ext[12 + at : 14 + at, :] = x - high
        out[EDGE:, :] = ext[...].astype(BF16)
        for s in range(OWN):
            for r in range(HALO):
                at = (r * OWN + s) * CH
                x = jnp.where(last, wide[s, :, TR - HALO + r, :], wide[s, :, r, :])
                out[at : at + CH, :] = x.astype(BF16)


def edges(*args):
    return call(
        edges_kernel,
        [
            ((EDGE_ALL, COLS), BF16),
            ((EDGE_ALL, COLS), BF16),
            ((OWN, CH, TR, COLS), F32),
            ((OWN, 2, TR, COLS), F32),
            ((OWN + 1, 8, COLS), F32),
        ],
        [
            (pltpu.SMEM, (OWN,), jnp.int32),
            (pltpu.SMEM, (OWN,), F32),
            (pltpu.SMEM, (2,), F32),
            ((OWN, CH, TR, COLS), BF16),
            ((OWN, 2, TR, COLS), F32),
            ((32, COLS), F32),
            (sems, (5,), None),
        ],
        3,
        "edges",
        "hhhhh",
        *args,
    )


def weights_kernel(
    k1_hbm, k2_hbm, b1_hbm, wcur, wear, wboth, w2own, w2first, w2rest, w2b, w2brest, wgear, wgcur, wgboth, bias,
    k1, k2, b1, fwd, bwd, both, two, sq, sems,
):
    fetch(sems, (k1_hbm, k1), (k2_hbm, k2), (b1_hbm, b1))
    bias[...] = jnp.broadcast_to(b1[...], (COLS, HID)).T
    for dy in range(3):
        for dx in range(3):
            k = k1[dy, dx].astype(F32)
            t = CH * (3 * dy + dx)
            fwd[0:HID, t : t + CH] = k[:, :CH]
            fwd[HID:, t : t + CH] = k[:, CH:]
            kt = k.T
            rows = slice(CH * dx, CH * dx + CH)
            bwd[rows, HID * dy : HID * dy + HID] = kt[:CH]
            bwd[3 * CH + CH * dx : 4 * CH + CH * dx, HID * dy : HID * dy + HID] = kt[CH:]
            both[rows, 2 * HID * dy : 2 * HID * dy + HID] = kt[:CH]
            both[rows, 2 * HID * dy + HID : 2 * HID * dy + 2 * HID] = kt[CH:]
    wcur[...] = fwd[0:HID, :].astype(BF16)
    wear[...] = fwd[HID:, :].astype(BF16)
    wboth[...] = fwd[...].astype(BF16)
    wgcur[...] = bwd[0 : 3 * CH, :].astype(BF16)
    wgear[...] = bwd[3 * CH :, :].astype(BF16)
    wgboth[...] = both[...].astype(BF16)

    def put(ref, row, col, lags):
        for i, lag in enumerate(lags):
            for dy in range(3):
                for dx in range(3):
                    at = row + 8 * (3 * dy + dx) + 2 * lag
                    c = col + HID * i
                    ref[at : at + 2, c : c + HID] = k2[dy, dx].astype(F32)

    two[...] = jnp.zeros(two.shape, F32)
    put(two, 0, 0, (0, 1, 2))
    w2first[...] = two[0:72, :].astype(BF16)
    two[...] = jnp.zeros(two.shape, F32)
    put(two, 0, 0, (1, 2))
    put(two, 72, 2 * HID, (2,))
    w2rest[...] = two[...].astype(BF16)
    two[...] = jnp.zeros(two.shape, F32)
    put(two, 0, 0, (0,))
    put(two, 72, HID, (0, 1))
    w2own[...] = two[...].astype(BF16)

    def lay(row, col, lags):
        for i, lag in enumerate(lags):
            for dy in range(3):
                for dx in range(3):
                    at = row + 32 * dy + 8 * dx + 2 * lag
                    c = col + HID * i
                    sq[at : at + 2, c : c + HID] = k2[dy, dx].astype(F32)

    sq[...] = jnp.zeros(sq.shape, F32)
    lay(0, 0, (0, 1, 2))
    w2b[...] = sq[0:96, :].T.astype(BF16)
    sq[...] = jnp.zeros(sq.shape, F32)
    lay(0, 0, (1, 2))
    lay(96, 2 * HID, (2,))
    w2brest[...] = sq[...].T.astype(BF16)


def weights(k1, k2, b1):
    return call(
        weights_kernel,
        [
            ((HID, 9 * CH), BF16),
            ((HID, 9 * CH), BF16),
            ((2 * HID, 9 * CH), BF16),
            ((144, 192), BF16),
            ((72, 192), BF16),
            ((144, 192), BF16),
            ((192, 96), BF16),
            ((192, 192), BF16),
            ((3 * CH, 3 * HID), BF16),
            ((3 * CH, 3 * HID), BF16),
            ((3 * CH, 6 * HID), BF16),
            ((HID, COLS), F32),
        ],
        [
            (k1.shape, BF16),
            (k2.shape, BF16),
            (b1.shape, F32),
            ((2 * HID, 9 * CH), F32),
            ((6 * CH, 3 * HID), F32),
            ((3 * CH, 6 * HID), F32),
            ((144, 192), F32),
            ((192, 192), F32),
            (sems, (3,), None),
        ],
        4,
        "weights",
        "hhh",
        k1,
        k2,
        b1,
    )


def spread_row(x, xd, j, r):
    xd[j, r, 0:CH, :] = from_left(x).astype(BF16)
    xd[j, r, CH : 2 * CH, :] = x.astype(BF16)
    xd[j, r, 2 * CH :, :] = from_right(x).astype(BF16)


def spread_own(wide, keep, xd):
    for s in range(OWN):
        for r in range(TR):
            x = wide[s, :, r, :]
            spread_row(x if keep is None else x * keep, xd, s, r)


def spread_rim(pick, scale, xr):
    for s in range(OWN):
        for r in range(HALO):
            for side in range(2):
                spread_row(pick(side, s, r) * scale[side], xr, s, HALO * side + r)


def feature_rows(xd, xr):
    def pick(j, r):
        if r < HALO:
            return xr[j, r]
        if r < HALO + TR:
            return xd[j, r - HALO]
        return xr[j, r - TR]

    return pick


def taps(rows, pick):
    return jnp.concatenate(
        [jnp.concatenate([pick(r), pick(r + 1)], axis=1) for r in rows], axis=0
    )


def halves(ref, r, first, x):
    n = x.shape[0]
    ref[r, first : first + n, :] = x[:, :COLS]
    ref[r + 1, first : first + n, :] = x[:, COLS:]


def pair_row(ref, r, first, n):
    return jnp.concatenate(
        [ref[r, first : first + n, :], ref[r + 1, first : first + n, :]], axis=1
    )


def gather_columns(p):
    return from_right(p[:CH]) + p[CH : 2 * CH] + from_left(p[2 * CH :])


def hidden_own(pairs, pick, wcur, wboth, bias, w2own, cur, hown, town):
    b = jnp.concatenate([bias[...], bias[...]], axis=1)
    for r in pairs:
        rhs = [taps((r, r + 1, r + 2), lambda q, j=j: pick(j, q)) for j in range(OWN)]
        both = [dot(wboth[...], rhs[j]) for j in range(2)]
        c = [both[0][:HID] + b, both[1][:HID] + b, dot(wcur[...], rhs[2]) + b]
        ear = [both[0][HID:], both[1][HID:]]
        for s in range(OWN):
            cur.put(r, HID * s, c[s])
        h = jnp.concatenate(
            [jnp.maximum(x, 0.0) for x in (c[1] + ear[0], c[2] + ear[1], c[2] + ear[0])], axis=0
        ).astype(BF16)
        hown.put(r, 0, h)
        town.put(r, 0, dot(w2own[...], h))


def hidden_borrowed(pairs, pick, wear, w2first, w2rest, cur, town, hmid, tsum):
    for r in pairs:
        ear = [
            dot(wear[...], taps((r, r + 1, r + 2), lambda q, j=j: pick(j, q)))
            for j in range(OWN)
        ]
        c = [cur.pair(r, HID * s, HID) for s in range(OWN)]
        h = [
            jnp.concatenate([jnp.maximum(c[s] + ear[3 + s - k], 0.0) for s, k in part], axis=0)
            for part in (((0, 1), (0, 2), (0, 3)), ((1, 2), (1, 3), (2, 3)))
        ]
        h = [x.astype(BF16) for x in h]
        hmid.put(r, 0, h[0])
        hmid.put(r, 192, h[1])
        tsum.put(r, 0, dot(w2first[...], h[0]))
        tsum.put(r, 72, dot(w2rest[...], h[1]) + town.pair(r, 0, 144))


def own_kernel(wide, wcur, wboth, bias, w2own, xd, cur, hown, town):
    spread_own(wide, None, xd)
    hidden_own(
        INNER_PAIRS, feature_rows(xd, None), wcur, wboth, bias, w2own,
        Rows(cur, None), Rows(hown, None), Rows(town, None),
    )


def hidden_outs(n):
    return [
        ((n, OWN * HID, COLS), F32),
        ((n, 3 * HID, COLS), BF16),
        ((n, 144, COLS), F32),
    ]


def own_inner(*args):
    return call(
        own_kernel,
        [((OWN, TR, 3 * CH, COLS), BF16)] + hidden_outs(INNER),
        [],
        2,
        "own_inner",
        "v" * len(args),
        *args,
    )


def rim_kernel(
    sibling, outer, cot16, xd, wcur, wboth, bias, w2own, rcur, rhown, rtown, rcot, xr
):
    odd = odd_tile()
    has = has_tiles()

    def halo(side, first, n):
        x, y = sibling[first : first + n, :], outer[first : first + n, :]
        x, y = x.astype(F32), y.astype(F32)
        return jnp.where(odd, x, y) if side == 0 else jnp.where(odd, y, x)

    for side, first in ((0, 0), (1, 6)):
        ext = halo(side, EDGE, 32) * has[side]
        for s in range(OWN):
            for c in range(2):
                at = s * 4 + c * 2
                rcot[s, c, first : first + 2, :] = ext[at : at + 2] + ext[12 + at : 14 + at]
    for s in range(OWN):
        for c in range(2):
            rcot[s, c, 2:4, :] = cot16[s, c, 0:2, :]
            rcot[s, c, 4:6, :] = cot16[s, c, TR - 2 :, :]
    spread_rim(lambda side, s, r: halo(side, (r * OWN + s) * CH, CH), has, xr)
    hidden_own(
        RIM_PAIRS, feature_rows(xd, xr), wcur, wboth, bias, w2own,
        Rows(None, rcur), Rows(None, rhown), Rows(None, rtown),
    )


def own_rim(*args):
    return call(
        rim_kernel,
        hidden_outs(RIM) + [((OWN, 2, 8, COLS), F32)],
        [((OWN, 2 * HALO, 3 * CH, COLS), BF16)],
        2,
        "own_rim",
        "v" * len(args),
        *args,
    )


def middle_kernel(
    prev, icur, itown, cot16, consts, wear, w2first, w2rest, w2b, w2brest, wgear,
    low, xp, ihmid, itsum, ig3, ivotes, idlow,
    wide, fld, grd,
):
    keep = (lax.axis_index("sec") > 0).astype(F32)
    for s in range(OWN):
        wide[s] = prev[s].astype(F32)
    spread_own(wide, keep, xp)
    hmid, tsum = Rows(ihmid, None), Rows(itsum, None)
    hidden_borrowed(
        INNER_PAIRS, feature_rows(xp, None), wear, w2first, w2rest,
        Rows(icur, None), Rows(itown, None), hmid, tsum,
    )
    fields_stage(inner_rows(FLD_INNER), tsum, consts.at[OWN], None, fld)
    vote_stage(
        FLD_INNER, consts, lambda s, c: cot16[s, c, 2 : TR - 2, :], fld, grd, ig3, ivotes
    )
    dlow = Rows(idlow, None, DH_INNER)
    low_grad_stage(
        inner_rows(DH_INNER, 2), w2b, w2brest, grad_rows(ig3, None), hmid, dlow
    )
    low_stage(inner_rows(OUT_INNER, 2), wgear, dlow, Rows(low, None, OUT_INNER))


def middle(*args):
    return call(
        middle_kernel,
        [
            ((OUT_INNER, OWN, CH, COLS), BF16),
            ((OWN, TR, 3 * CH, COLS), BF16),
            ((INNER, 6 * HID, COLS), BF16),
            ((INNER, OWN * 72, COLS), F32),
            ((OWN, FLD_INNER, 32, COLS), BF16),
            ((OWN, 2, 16, COLS), F32),
            ((DH_INNER, 3 * HID, COLS), BF16),
        ],
        [
            ((OWN, CH, TR, COLS), F32),
            ((OWN, FLD_INNER, 8, COLS), F32),
            ((OWN, FLD_INNER, 8, COLS), F32),
        ],
        4,
        "middle",
        "v" * len(args),
        *args,
    )


def fields_stage(rows, tsum, bias2, has, fld):
    for i, r in enumerate(rows):
        for s in range(OWN):
            sums = []
            for dx in range(3):
                terms = []
                for dy in range(3):
                    at = 72 * s + 8 * (3 * dy + dx)
                    ref, j = tsum.at(r + dy)
                    t = ref[j, at : at + 8, :]
                    if r + dy < 3:
                        t = t * has[0]
                    elif r + dy > HID_ROWS - 4:
                        t = t * has[1]
                    terms.append(t)
                sums.append(terms[0] + terms[1] + terms[2])
            fld[s, i] = (sums[1] + bias2[...]) + (from_left(sums[0]) + from_right(sums[2]))


def vote_stage(n, consts, cot_of, fld, grd, g3, votes):
    for s in range(OWN):
        f = [[fld[s, :, 2 * k + c, :] for c in range(2)] for k in range(3)]
        beta = consts[s, 0:1, :]
        diff = {}
        dist = {}
        for a, b in ((0, 1), (0, 2), (1, 2)):
            diff[a, b] = [f[a][c] - f[b][c] for c in range(2)]
            dist[a, b] = diff[a, b][0] * diff[a, b][0] + diff[a, b][1] * diff[a, b][1]
        score = [dist[0, 1] + dist[0, 2], dist[0, 1] + dist[1, 2], dist[0, 2] + dist[1, 2]]
        logit = [-beta * q for q in score]
        top = jnp.maximum(jnp.maximum(logit[0], logit[1]), logit[2])
        expo = [jnp.exp(q - top) for q in logit]
        inv = 1.0 / (expo[0] + expo[1] + expo[2])
        w = [q * inv for q in expo]
        v = [w[0] * f[0][c] + w[1] * f[1][c] + w[2] * f[2][c] for c in range(2)]
        for c in range(2):
            votes[s, c, 0:n, :] = v[c]
        g = [cot_of(s, c) for c in range(2)]
        e = [
            -beta * w[k] * (g[0] * (f[k][0] - v[0]) + g[1] * (f[k][1] - v[1])) for k in range(3)
        ]
        pair = {key: 2.0 * (e[key[0]] + e[key[1]]) for key in diff}
        for c in range(2):
            m01 = pair[0, 1] * diff[0, 1][c]
            m02 = pair[0, 2] * diff[0, 2][c]
            m12 = pair[1, 2] * diff[1, 2][c]
            grd[s, :, 0 + c, :] = w[0] * g[c] + m01 + m02
            grd[s, :, 2 + c, :] = w[1] * g[c] - m01 + m12
            grd[s, :, 4 + c, :] = w[2] * g[c] - m02 - m12
        grd[s, :, 6, :] = jnp.zeros((n, COLS), F32)
        grd[s, :, 7, :] = jnp.zeros((n, COLS), F32)
    for r in range(n):
        for s in range(OWN):
            x = grd[s, r]
            g3[s, r] = jnp.concatenate(
                [from_right(x), x, from_left(x), jnp.zeros_like(x)], axis=0
            ).astype(BF16)


def inside(ref, has):
    for r, h in ((0, has[0]), (ref.shape[0] - 1, has[1])):
        ref[r] = (ref[r].astype(F32) * h).astype(BF16)


def low_grad_stage(rows, w2b, w2brest, g3, hmid, dlow):
    for q in rows:
        rhs = [taps((q + 2, q + 1, q), lambda r, s=s: g3(s, r)) for s in range(OWN)]
        h = [hmid.pair(q + 2, 192 * j, 192).astype(F32) for j in range(2)]
        first = jnp.where(h[0] > 0.0, dot(w2b[...], rhs[0]), 0.0)
        rest = jnp.where(
            h[1] > 0.0, dot(w2brest[...], jnp.concatenate([rhs[1], rhs[2]], axis=0)), 0.0
        )
        low = jnp.concatenate(
            [
                first[2 * HID :],
                first[HID : 2 * HID] + rest[HID : 2 * HID],
                first[:HID] + rest[:HID] + rest[2 * HID :],
            ],
            axis=0,
        ).astype(BF16)
        dlow.put(q, 0, low)


def low_stage(rows, wgear, dlow, low):
    for r in rows:
        for s in range(OWN):

            def pick(q, s=s):
                ref, i = dlow.at(q)
                return ref[i, HID * s : HID * s + HID, :]

            p = dot(wgear[...], taps((r + 2, r + 1, r), pick))
            for d in range(2):
                ref, i = low.at(r + d)
                ref[i, s] = gather_columns(p[:, COLS * d : COLS * d + COLS]).astype(BF16)


def grad_rows(ig3, rg3):
    rows = Rows(ig3, rg3, FLD_INNER)

    def pick(s, r):
        ref, i = rows.at(r)
        return ref[s, i]

    return pick


def feature_grad_stage(dref, jobs, unroll):
    def step(i, carry):
        r = 2 * i
        for first, size, weight, out, s in jobs:
            rhs = taps((r + 2, r + 1, r), lambda q: dref[q, first : first + size, :])
            p = dot(weight[...], rhs)
            for d in range(2):
                out[r + d, s] = gather_columns(p[:, COLS * d : COLS * d + COLS]).astype(out.dtype)
        return carry

    lax.fori_loop(0, TR // 2, step, 0, unroll=unroll)


def borrowed_kernel(
    psib, pouter, xp, rcur, rtown, itsum, ihmid, ig3, idlow, rcot, consts,
    wear, w2first, w2rest, w2b, w2brest, wgear,
    low, rhmid, rg3, rvotes,
    wide, xr, rtsum, fld, grd, rdlow,
):
    odd = odd_tile()
    has = has_tiles()
    keep = (lax.axis_index("sec") > 0).astype(F32)
    for s in range(OWN):
        wide[s] = psib[s].astype(F32)

    def halo(side, s, r):
        at = (r * OWN + s) * CH
        y = pouter[at : at + CH, :].astype(F32)
        if side == 0:
            return jnp.where(odd, wide[s, :, TR - HALO + r, :], y)
        return jnp.where(odd, y, wide[s, :, r, :])

    spread_rim(halo, [keep * h for h in has], xr)
    hmid, tsum = Rows(ihmid, rhmid), Rows(itsum, rtsum)
    hidden_borrowed(
        RIM_PAIRS, feature_rows(xp, xr), wear, w2first, w2rest,
        Rows(None, rcur), Rows(None, rtown), hmid, tsum,
    )
    fields_stage(rim_rows(FLD_INNER), tsum, consts.at[OWN], has, fld)
    vote_stage(2 * HALO, consts, lambda s, c: rcot[s, c], fld, grd, rg3, rvotes)
    dlow = Rows(idlow, rdlow, DH_INNER)
    low_grad_stage(rim_rows(DH_INNER, 2), w2b, w2brest, grad_rows(ig3, rg3), hmid, dlow)
    inside(rdlow, has)
    low_stage(rim_rows(OUT_INNER, 2), wgear, dlow, Rows(None, low, OUT_INNER))


def borrowed(*args):
    return call(
        borrowed_kernel,
        [
            ((2 * HALO, OWN, CH, COLS), BF16),
            ((RIM, 6 * HID, COLS), BF16),
            ((OWN, 2 * HALO, 32, COLS), BF16),
            ((OWN, 2, 8, COLS), F32),
        ],
        [
            ((OWN, CH, TR, COLS), F32),
            ((OWN, 2 * HALO, 3 * CH, COLS), BF16),
            ((RIM, OWN * 72, COLS), F32),
            ((OWN, 2 * HALO, 8, COLS), F32),
            ((OWN, 2 * HALO, 8, COLS), F32),
            ((2 * HALO, 3 * HID, COLS), BF16),
        ],
        6,
        "borrowed",
        "v" * len(args),
        *args,
    )


def own_grad_kernel(
    ivotes, rvotes, ig3, rg3, ihown, rhown, ihmid, rhmid, w2b, wgcur, wgboth, voted, grad, down
):
    has = has_tiles()
    hown, hmid = Rows(ihown, rhown), Rows(ihmid, rhmid)
    g3 = grad_rows(ig3, rg3)
    for s in range(OWN):
        for c in range(2):
            voted[s, c, 0:2, :] = rvotes[s, c, 2:4, :]
            voted[s, c, 2 : TR - 2, :] = ivotes[s, c, 0:FLD_INNER, :]
            voted[s, c, TR - 2 :, :] = rvotes[s, c, 4:6, :]
    for q in range(0, DH_ROWS, 2):
        ho = hown.pair(q + 2, 0, 192)
        hm = hmid.pair(q + 2, 0, 384)
        h = [
            hm[:192],
            jnp.concatenate([ho[:64], hm[192:320]], axis=0),
            jnp.concatenate([ho[64:], hm[320:]], axis=0),
        ]
        m = []
        for s in range(OWN):
            dh = dot(w2b[...], taps((q + 2, q + 1, q), lambda r, s=s: g3(s, r)))
            dh = jnp.where(h[s].astype(F32) > 0.0, dh, 0.0)
            m.append([dh[HID * k : HID * k + HID] for k in range(3)])
        c = [m[s][0] + m[s][1] + m[s][2] for s in range(OWN)]
        d = jnp.concatenate([c[0], m[1][0] + m[2][1], c[1], m[2][0], c[2]], axis=0).astype(BF16)
        halves(down, q, 0, d)
    inside(down, has)
    feature_grad_stage(
        down,
        [(0, 128, wgboth, grad, 0), (128, 128, wgboth, grad, 1), (256, 64, wgcur, grad, 2)],
        4,
    )


def own_grad(*args):
    return call(
        own_grad_kernel,
        [((OWN, 2, TR, COLS), F32), ((TR, OWN, CH, COLS), F32)],
        [((DH_ROWS, 5 * HID, COLS), BF16)],
        4,
        "own_grad",
        "v" * len(args),
        *args,
    )


def finish_kernel(grad, iback, rback, out, block, sems):
    keep = (lax.axis_index("sec") < lax.axis_size("sec") - 1).astype(F32)
    back = Rows(iback, rback, OUT_INNER)
    copies = []
    for s in range(OWN):
        for r in range(TR):
            ref, i = back.at(r)
            block[s, :, r, :] = grad[r, s] + ref[i, s].astype(F32) * keep
        copies.append(pltpu.make_async_copy(block.at[s], out.at[s], sems.at[s]))
        copies[-1].start()
    for c in copies:
        c.wait()


def finish(*args):
    vmem = pl.BlockSpec(memory_space=pltpu.VMEM)
    return pl.pallas_call(
        finish_kernel,
        out_shape=jax.ShapeDtypeStruct((OWN, CH, TR, COLS), F32),
        in_specs=[vmem] * len(args),
        out_specs=pl.BlockSpec(memory_space=pltpu.HBM),
        scratch_shapes=[
            pltpu.VMEM((OWN, CH, TR, COLS), F32),
            pltpu.SemaphoreType.DMA((OWN,)),
        ],
        compiler_params=params(2),
        name="finish",
    )(*args)


def move(value, secs, tile_to, wrap=True):
    n, m = lax.axis_size("sec"), lax.axis_size("tile")
    pairs = [
        (a * m + b, ((a + secs) % n) * m + tile_to(b))
        for a in range(n)
        for b in range(m)
        if tile_to(b) is not None and (wrap or 0 <= a + secs < n)
    ]
    return lax.ppermute(value, ("sec", "tile"), pairs)


def body(
    features, vote_grad, sharpness, valid_rows, first_kernel, first_bias, second_kernel, second_bias
):
    tiles = lax.axis_size("tile")

    def same(b):
        return b

    def to_sibling(b):
        return b + 1 - 2 * (b % 2)

    def to_outer(b):
        other = b - 1 + 2 * (b % 2)
        return other if 0 <= other < tiles else None

    prev = move(features, 1, same)
    for_sibling, for_outer, wide, cot16, consts = edges(
        valid_rows, sharpness, second_bias, features, vote_grad
    )
    sibling = move(for_sibling, 0, to_sibling)
    outer = move(for_outer, 0, to_outer)
    pouter = move(for_outer, 1, to_outer, False)
    (
        wcur, wear, wboth, w2own, w2first, w2rest, w2b, w2brest, wgear, wgcur, wgboth, bias,
    ) = weights(first_kernel, second_kernel, first_bias[None])
    xd, icur, ihown, itown = own_inner(wide, wcur, wboth, bias, w2own)
    rcur, rhown, rtown, rcot = own_rim(
        sibling, outer, cot16, xd, wcur, wboth, bias, w2own
    )
    prev, rcur, pouter = lax.optimization_barrier((prev, rcur, pouter))
    psib = move(prev, 0, to_sibling)
    ilow, xp, ihmid, itsum, ig3, ivotes, idlow = middle(
        prev, icur, itown, cot16, consts, wear, w2first, w2rest, w2b, w2brest, wgear
    )
    iback = move(ilow, -1, same)
    rlow, rhmid, rg3, rvotes = borrowed(
        psib, pouter, xp, rcur, rtown, itsum, ihmid, ig3, idlow, rcot, consts,
        wear, w2first, w2rest, w2b, w2brest, wgear,
    )
    rback = move(rlow, -1, same)
    voted, grad = own_grad(
        ivotes, rvotes, ig3, rg3, ihown, rhown, ihmid, rhmid, w2b, wgcur, wgboth
    )
    return (voted, finish(grad, iback, rback))


def solution(mesh):
    return jax.shard_map(
        body,
        mesh=mesh,
        in_specs=(
            P("sec", None, "tile", None),
            P("sec", None, "tile", None),
            P("sec"),
            P("sec"),
            P(),
            P(),
            P(),
            P(),
        ),
        out_specs=(P("sec", None, "tile", None), P("sec", None, "tile", None)),
        check_vma=False,
    )
```

```python
import jax
import jax.numpy as jnp
from jax import lax
from jax.experimental import pallas as pl
from jax.experimental.pallas import tpu as pltpu
from jax.sharding import PartitionSpec as P

F32 = jnp.float32
BF16 = jnp.bfloat16
OWN = 3
CH = 32
HID = 64
TR = 16
COLS = 128
HALO = 4
FEAT_ROWS = TR + 2 * HALO
HID_ROWS = FEAT_ROWS - 2
FLD_ROWS = FEAT_ROWS - 4
DH_ROWS = FEAT_ROWS - 6
EDGE = HALO * OWN * CH
EDGE_ALL = EDGE + 32


def lane(shape):
    return lax.broadcasted_iota(jnp.int32, shape, len(shape) - 1)


def from_left(x):
    return jnp.where(lane(x.shape) == 0, 0.0, pltpu.roll(x, 1, x.ndim - 1))


def from_right(x):
    return jnp.where(lane(x.shape) == COLS - 1, 0.0, pltpu.roll(x, COLS - 1, x.ndim - 1))


def dot(a, b):
    return jnp.dot(a, b, preferred_element_type=F32)


def params(mib):
    return pltpu.CompilerParams(vmem_limit_bytes=mib << 20)


COST = {
    "own_rim": 0,
    "edges": 0,
    "weights": 0,
    "own_inner": 0,
    "middle": 2306,
    "borrowed": 3459,
    "own_grad": 3459,
    "finish": 1153,
}
INNER = TR - 2
RIM = HID_ROWS - INNER
INNER_PAIRS = [HALO + 2 * i for i in range(INNER // 2)]
RIM_PAIRS = [0, 2, HALO + INNER, HALO + INNER + 2]
FLD_INNER = FLD_ROWS - 2 * HALO
DH_INNER = DH_ROWS - 2 * HALO
OUT_INNER = TR - 2 * HALO


def inner_rows(count, step=1):
    return range(HALO, HALO + count, step)


def rim_rows(count, step=1):
    return [*range(0, HALO, step), *range(HALO + count, 2 * HALO + count, step)]


def call(kernel, outs, scratch, mib, name, specs, *args):
    space = {"v": pltpu.VMEM, "h": pltpu.HBM}
    args = [
        pltpu.with_memory_space_constraint(x, pltpu.HBM) if c == "h" else x
        for x, c in zip(args, specs, strict=True)
    ]
    return pl.pallas_call(
        kernel,
        out_shape=tuple(jax.ShapeDtypeStruct(shape, kind) for shape, kind in outs),
        in_specs=[pl.BlockSpec(memory_space=space[c]) for c in specs],
        out_specs=(pl.BlockSpec(memory_space=pltpu.VMEM),) * len(outs),
        scratch_shapes=[
            item[0](item[1], item[2]) if len(item) == 3 else pltpu.VMEM(*item) for item in scratch
        ],
        compiler_params=params(mib),
        cost_estimate=pl.CostEstimate(
            flops=COST[name] * 10**6, bytes_accessed=0, transcendentals=0
        ),
        name=name,
    )(*args)


def sems(shape, _):
    return pltpu.SemaphoreType.DMA(shape)


def fetch(sems, *moves):
    copies = [pltpu.make_async_copy(a, b, sems.at[i]) for i, (a, b) in enumerate(moves)]
    for c in copies:
        c.start()
    return copies


def odd_tile():
    return lax.axis_index("tile") % 2 == 1


def has_tiles():
    tile = lax.axis_index("tile")
    return (tile > 0).astype(F32), (tile < lax.axis_size("tile") - 1).astype(F32)


class Rows:
    def __init__(self, inner, rim, count=INNER):
        self.inner, self.rim, self.count = inner, rim, count

    def at(self, r):
        if r < HALO:
            return self.rim, r
        if r < HALO + self.count:
            return self.inner, r - HALO
        return self.rim, r - self.count

    def pair(self, r, first, n):
        ref, i = self.at(r)
        return pair_row(ref, i, first, n)

    def put(self, r, first, x):
        ref, i = self.at(r)
        halves(ref, i, first, x)


def edges_kernel(
    valid_hbm, sharp_hbm, b2_hbm, feat_hbm, vgrad_hbm, k1_hbm, k2_hbm, b1_hbm,
    sibling, outer, wide, cot, consts, k1, k2, b1,
    valid, sharp, b2, feat, vgrad, ext, sems,
):
    copies = fetch(
        sems,
        (feat_hbm, feat), (vgrad_hbm, vgrad), (valid_hbm, valid), (sharp_hbm, sharp), (b2_hbm, b2),
        (k1_hbm, k1), (k2_hbm, k2), (b1_hbm, b1),
    )
    for c in copies[:5]:
        c.wait()
    row0 = lax.axis_index("tile") * TR
    odd = odd_tile()
    for s in range(OWN):
        wide[s] = feat[s].astype(F32)
        pos = row0 + lax.broadcasted_iota(jnp.int32, (TR, COLS), 0)
        for c in range(2):
            cot[s, c] = jnp.where(pos < valid[s], vgrad[s, c], 0.0)
        consts[s] = jnp.full((8, COLS), sharp[s], F32)
    even_row = lax.broadcasted_iota(jnp.int32, (8, COLS), 0) % 2 == 0
    consts[OWN] = jnp.where(even_row, b2[0], b2[1])
    for out, last in ((sibling, jnp.logical_not(odd)), (outer, odd)):
        ext[...] = jnp.zeros((32, COLS), F32)
        for s in range(OWN):
            for c in range(2):
                x = jnp.where(last, cot[s, c, TR - 2 :, :], cot[s, c, 0:2, :])
                high = x.astype(BF16).astype(F32)
                at = s * 4 + c * 2
                ext[at : at + 2, :] = high
                ext[12 + at : 14 + at, :] = x - high
        out[EDGE:, :] = ext[...].astype(BF16)
    for s in range(OWN):
        for r in range(HALO):
            at = (r * OWN + s) * CH
            top, bottom = wide[s, :, r, :], wide[s, :, TR - HALO + r, :]
            sibling[at : at + CH, :] = jnp.where(odd, top, bottom).astype(BF16)
            outer[at : at + CH, :] = jnp.where(odd, bottom, top).astype(BF16)
    for c in copies[5:]:
        c.wait()


def edges(*args):
    k1, k2, b1 = args[5:]
    return call(
        edges_kernel,
        [
            ((EDGE_ALL, COLS), BF16),
            ((EDGE_ALL, COLS), BF16),
            ((OWN, CH, TR, COLS), F32),
            ((OWN, 2, TR, COLS), F32),
            ((OWN + 1, 8, COLS), F32),
            (k1.shape, BF16),
            (k2.shape, BF16),
            (b1.shape, F32),
        ],
        [
            (pltpu.SMEM, (OWN,), jnp.int32),
            (pltpu.SMEM, (OWN,), F32),
            (pltpu.SMEM, (2,), F32),
            ((OWN, CH, TR, COLS), BF16),
            ((OWN, 2, TR, COLS), F32),
            ((32, COLS), F32),
            (sems, (8,), None),
        ],
        3,
        "edges",
        "hhhhhhhh",
        *args,
    )


def weights_kernel(
    k1, k2, b1, wcur, wear, wboth, w2own, w2first, w2rest, w2b, w2brest, wgear, wgcur, wgboth, bias,
    fwd, bwd, both, two, sq,
):
    bias[...] = jnp.broadcast_to(b1[...], (COLS, HID)).T
    for dy in range(3):
        for dx in range(3):
            k = k1[dy, dx].astype(F32)
            t = CH * (3 * dy + dx)
            fwd[0:HID, t : t + CH] = k[:, :CH]
            fwd[HID:, t : t + CH] = k[:, CH:]
            kt = k.T
            rows = slice(CH * dx, CH * dx + CH)
            bwd[rows, HID * dy : HID * dy + HID] = kt[:CH]
            bwd[3 * CH + CH * dx : 4 * CH + CH * dx, HID * dy : HID * dy + HID] = kt[CH:]
            both[rows, 2 * HID * dy : 2 * HID * dy + HID] = kt[:CH]
            both[rows, 2 * HID * dy + HID : 2 * HID * dy + 2 * HID] = kt[CH:]
    wcur[...] = fwd[0:HID, :].astype(BF16)
    wear[...] = fwd[HID:, :].astype(BF16)
    wboth[...] = fwd[...].astype(BF16)
    wgcur[...] = bwd[0 : 3 * CH, :].astype(BF16)
    wgear[...] = bwd[3 * CH :, :].astype(BF16)
    wgboth[...] = both[...].astype(BF16)

    def put(ref, row, col, lags):
        for i, lag in enumerate(lags):
            for dy in range(3):
                for dx in range(3):
                    at = row + 8 * (3 * dy + dx) + 2 * lag
                    c = col + HID * i
                    ref[at : at + 2, c : c + HID] = k2[dy, dx].astype(F32)

    two[...] = jnp.zeros(two.shape, F32)
    put(two, 0, 0, (0, 1, 2))
    w2first[...] = two[0:72, :].astype(BF16)
    two[...] = jnp.zeros(two.shape, F32)
    put(two, 0, 0, (1, 2))
    put(two, 72, 2 * HID, (2,))
    w2rest[...] = two[...].astype(BF16)
    two[...] = jnp.zeros(two.shape, F32)
    put(two, 0, 0, (0,))
    put(two, 72, HID, (0, 1))
    w2own[...] = two[...].astype(BF16)

    def lay(row, col, lags):
        for i, lag in enumerate(lags):
            for dy in range(3):
                for dx in range(3):
                    at = row + 32 * dy + 8 * dx + 2 * lag
                    c = col + HID * i
                    sq[at : at + 2, c : c + HID] = k2[dy, dx].astype(F32)

    sq[...] = jnp.zeros(sq.shape, F32)
    lay(0, 0, (0, 1, 2))
    w2b[...] = sq[0:96, :].T.astype(BF16)
    sq[...] = jnp.zeros(sq.shape, F32)
    lay(0, 0, (1, 2))
    lay(96, 2 * HID, (2,))
    w2brest[...] = sq[...].T.astype(BF16)


def weights(k1, k2, b1):
    return call(
        weights_kernel,
        [
            ((HID, 9 * CH), BF16),
            ((HID, 9 * CH), BF16),
            ((2 * HID, 9 * CH), BF16),
            ((144, 192), BF16),
            ((72, 192), BF16),
            ((144, 192), BF16),
            ((192, 96), BF16),
            ((192, 192), BF16),
            ((3 * CH, 3 * HID), BF16),
            ((3 * CH, 3 * HID), BF16),
            ((3 * CH, 6 * HID), BF16),
            ((HID, COLS), F32),
        ],
        [
            ((2 * HID, 9 * CH), F32),
            ((6 * CH, 3 * HID), F32),
            ((3 * CH, 6 * HID), F32),
            ((144, 192), F32),
            ((192, 192), F32),
        ],
        4,
        "weights",
        "vvv",
        k1,
        k2,
        b1,
    )


def spread_row(x, xd, j, r):
    xd[j, r, 0:CH, :] = from_left(x).astype(BF16)
    xd[j, r, CH : 2 * CH, :] = x.astype(BF16)
    xd[j, r, 2 * CH :, :] = from_right(x).astype(BF16)


def spread_own(wide, keep, xd):
    for s in range(OWN):
        for r in range(TR):
            x = wide[s, :, r, :]
            spread_row(x if keep is None else x * keep, xd, s, r)


def spread_rim(pick, scale, xr):
    for s in range(OWN):
        for r in range(HALO):
            for side in range(2):
                spread_row(pick(side, s, r) * scale[side], xr, s, HALO * side + r)


def feature_rows(xd, xr):
    def pick(j, r):
        if r < HALO:
            return xr[j, r]
        if r < HALO + TR:
            return xd[j, r - HALO]
        return xr[j, r - TR]

    return pick


def taps(rows, pick):
    return jnp.concatenate(
        [jnp.concatenate([pick(r), pick(r + 1)], axis=1) for r in rows], axis=0
    )


def halves(ref, r, first, x):
    n = x.shape[0]
    ref[r, first : first + n, :] = x[:, :COLS]
    ref[r + 1, first : first + n, :] = x[:, COLS:]


def pair_row(ref, r, first, n):
    return jnp.concatenate(
        [ref[r, first : first + n, :], ref[r + 1, first : first + n, :]], axis=1
    )


def gather_columns(p):
    return from_right(p[:CH]) + p[CH : 2 * CH] + from_left(p[2 * CH :])


def hidden_own(pairs, pick, wcur, wboth, bias, w2own, cur, hown, town):
    b = jnp.concatenate([bias[...], bias[...]], axis=1)
    for r in pairs:
        rhs = [taps((r, r + 1, r + 2), lambda q, j=j: pick(j, q)) for j in range(OWN)]
        both = [dot(wboth[...], rhs[j]) for j in range(2)]
        c = [both[0][:HID] + b, both[1][:HID] + b, dot(wcur[...], rhs[2]) + b]
        ear = [both[0][HID:], both[1][HID:]]
        for s in range(OWN):
            cur.put(r, HID * s, c[s])
        h = jnp.concatenate(
            [jnp.maximum(x, 0.0) for x in (c[1] + ear[0], c[2] + ear[1], c[2] + ear[0])], axis=0
        ).astype(BF16)
        hown.put(r, 0, h)
        town.put(r, 0, dot(w2own[...], h))


def hidden_borrowed(pairs, pick, wear, w2first, w2rest, cur, town, hmid, tsum):
    for r in pairs:
        ear = [
            dot(wear[...], taps((r, r + 1, r + 2), lambda q, j=j: pick(j, q)))
            for j in range(OWN)
        ]
        c = [cur.pair(r, HID * s, HID) for s in range(OWN)]
        h = [
            jnp.concatenate([jnp.maximum(c[s] + ear[3 + s - k], 0.0) for s, k in part], axis=0)
            for part in (((0, 1), (0, 2), (0, 3)), ((1, 2), (1, 3), (2, 3)))
        ]
        h = [x.astype(BF16) for x in h]
        hmid.put(r, 0, h[0])
        hmid.put(r, 192, h[1])
        tsum.put(r, 0, dot(w2first[...], h[0]))
        tsum.put(r, 72, dot(w2rest[...], h[1]) + town.pair(r, 0, 144))


def own_kernel(wide, wcur, wboth, bias, w2own, xd, cur, hown, town):
    spread_own(wide, None, xd)
    hidden_own(
        INNER_PAIRS, feature_rows(xd, None), wcur, wboth, bias, w2own,
        Rows(cur, None), Rows(hown, None), Rows(town, None),
    )


def hidden_outs(n):
    return [
        ((n, OWN * HID, COLS), F32),
        ((n, 3 * HID, COLS), BF16),
        ((n, 144, COLS), F32),
    ]


def own_inner(*args):
    return call(
        own_kernel,
        [((OWN, TR, 3 * CH, COLS), BF16)] + hidden_outs(INNER),
        [],
        2,
        "own_inner",
        "v" * len(args),
        *args,
    )


def rim_kernel(
    sibling, outer, cot16, xd, wcur, wboth, bias, w2own, rcur, rhown, rtown, rcot, xr
):
    odd = odd_tile()
    has = has_tiles()

    def halo(side, first, n):
        x, y = sibling[first : first + n, :], outer[first : first + n, :]
        x, y = x.astype(F32), y.astype(F32)
        return jnp.where(odd, x, y) if side == 0 else jnp.where(odd, y, x)

    for side, first in ((0, 0), (1, 6)):
        ext = halo(side, EDGE, 32) * has[side]
        for s in range(OWN):
            for c in range(2):
                at = s * 4 + c * 2
                rcot[s, c, first : first + 2, :] = ext[at : at + 2] + ext[12 + at : 14 + at]
    for s in range(OWN):
        for c in range(2):
            rcot[s, c, 2:4, :] = cot16[s, c, 0:2, :]
            rcot[s, c, 4:6, :] = cot16[s, c, TR - 2 :, :]
    spread_rim(lambda side, s, r: halo(side, (r * OWN + s) * CH, CH), has, xr)
    hidden_own(
        RIM_PAIRS, feature_rows(xd, xr), wcur, wboth, bias, w2own,
        Rows(None, rcur), Rows(None, rhown), Rows(None, rtown),
    )


def own_rim(*args):
    return call(
        rim_kernel,
        hidden_outs(RIM) + [((OWN, 2, 8, COLS), F32)],
        [((OWN, 2 * HALO, 3 * CH, COLS), BF16)],
        2,
        "own_rim",
        "v" * len(args),
        *args,
    )


def middle_kernel(
    prev, icur, itown, cot16, consts, wear, w2first, w2rest, w2b, w2brest, wgear,
    low, xp, ihmid, itsum, ig3, ivotes, idlow,
    wide, fld, grd,
):
    keep = (lax.axis_index("sec") > 0).astype(F32)
    for s in range(OWN):
        wide[s] = prev[s].astype(F32)
    spread_own(wide, keep, xp)
    hmid, tsum = Rows(ihmid, None), Rows(itsum, None)
    hidden_borrowed(
        INNER_PAIRS, feature_rows(xp, None), wear, w2first, w2rest,
        Rows(icur, None), Rows(itown, None), hmid, tsum,
    )
    fields_stage(inner_rows(FLD_INNER), tsum, consts.at[OWN], None, fld)
    vote_stage(
        FLD_INNER, consts, lambda s, c: cot16[s, c, 2 : TR - 2, :], fld, grd, ig3, ivotes
    )
    dlow = Rows(idlow, None, DH_INNER)
    low_grad_stage(
        inner_rows(DH_INNER, 2), w2b, w2brest, grad_rows(ig3, None), hmid, dlow
    )
    low_stage(inner_rows(OUT_INNER, 2), wgear, dlow, Rows(low, None, OUT_INNER))


def middle(*args):
    return call(
        middle_kernel,
        [
            ((OUT_INNER, OWN, CH, COLS), BF16),
            ((OWN, TR, 3 * CH, COLS), BF16),
            ((INNER, 6 * HID, COLS), BF16),
            ((INNER, OWN * 72, COLS), F32),
            ((OWN, FLD_INNER, 32, COLS), BF16),
            ((OWN, 2, 16, COLS), F32),
            ((DH_INNER, 3 * HID, COLS), BF16),
        ],
        [
            ((OWN, CH, TR, COLS), F32),
            ((OWN, FLD_INNER, 8, COLS), F32),
            ((OWN, FLD_INNER, 8, COLS), F32),
        ],
        4,
        "middle",
        "v" * len(args),
        *args,
    )


def fields_stage(rows, tsum, bias2, has, fld):
    for i, r in enumerate(rows):
        for s in range(OWN):
            sums = []
            for dx in range(3):
                terms = []
                for dy in range(3):
                    at = 72 * s + 8 * (3 * dy + dx)
                    ref, j = tsum.at(r + dy)
                    t = ref[j, at : at + 8, :]
                    if r + dy < 3:
                        t = t * has[0]
                    elif r + dy > HID_ROWS - 4:
                        t = t * has[1]
                    terms.append(t)
                sums.append(terms[0] + terms[1] + terms[2])
            fld[s, i] = (sums[1] + bias2[...]) + (from_left(sums[0]) + from_right(sums[2]))


def vote_stage(n, consts, cot_of, fld, grd, g3, votes):
    for s in range(OWN):
        f = [[fld[s, :, 2 * k + c, :] for c in range(2)] for k in range(3)]
        beta = consts[s, 0:1, :]
        diff = {}
        dist = {}
        for a, b in ((0, 1), (0, 2), (1, 2)):
            diff[a, b] = [f[a][c] - f[b][c] for c in range(2)]
            dist[a, b] = diff[a, b][0] * diff[a, b][0] + diff[a, b][1] * diff[a, b][1]
        score = [dist[0, 1] + dist[0, 2], dist[0, 1] + dist[1, 2], dist[0, 2] + dist[1, 2]]
        logit = [-beta * q for q in score]
        top = jnp.maximum(jnp.maximum(logit[0], logit[1]), logit[2])
        expo = [jnp.exp(q - top) for q in logit]
        inv = 1.0 / (expo[0] + expo[1] + expo[2])
        w = [q * inv for q in expo]
        v = [w[0] * f[0][c] + w[1] * f[1][c] + w[2] * f[2][c] for c in range(2)]
        for c in range(2):
            votes[s, c, 0:n, :] = v[c]
        g = [cot_of(s, c) for c in range(2)]
        e = [
            -beta * w[k] * (g[0] * (f[k][0] - v[0]) + g[1] * (f[k][1] - v[1])) for k in range(3)
        ]
        pair = {key: 2.0 * (e[key[0]] + e[key[1]]) for key in diff}
        for c in range(2):
            m01 = pair[0, 1] * diff[0, 1][c]
            m02 = pair[0, 2] * diff[0, 2][c]
            m12 = pair[1, 2] * diff[1, 2][c]
            grd[s, :, 0 + c, :] = w[0] * g[c] + m01 + m02
            grd[s, :, 2 + c, :] = w[1] * g[c] - m01 + m12
            grd[s, :, 4 + c, :] = w[2] * g[c] - m02 - m12
        grd[s, :, 6, :] = jnp.zeros((n, COLS), F32)
        grd[s, :, 7, :] = jnp.zeros((n, COLS), F32)
    for r in range(n):
        for s in range(OWN):
            x = grd[s, r]
            g3[s, r] = jnp.concatenate(
                [from_right(x), x, from_left(x), jnp.zeros_like(x)], axis=0
            ).astype(BF16)


def inside(ref, has):
    for r, h in ((0, has[0]), (ref.shape[0] - 1, has[1])):
        ref[r] = (ref[r].astype(F32) * h).astype(BF16)


def low_grad_stage(rows, w2b, w2brest, g3, hmid, dlow):
    for q in rows:
        rhs = [taps((q + 2, q + 1, q), lambda r, s=s: g3(s, r)) for s in range(OWN)]
        h = [hmid.pair(q + 2, 192 * j, 192).astype(F32) for j in range(2)]
        first = jnp.where(h[0] > 0.0, dot(w2b[...], rhs[0]), 0.0)
        rest = jnp.where(
            h[1] > 0.0, dot(w2brest[...], jnp.concatenate([rhs[1], rhs[2]], axis=0)), 0.0
        )
        low = jnp.concatenate(
            [
                first[2 * HID :],
                first[HID : 2 * HID] + rest[HID : 2 * HID],
                first[:HID] + rest[:HID] + rest[2 * HID :],
            ],
            axis=0,
        ).astype(BF16)
        dlow.put(q, 0, low)


def low_stage(rows, wgear, dlow, low):
    for r in rows:
        for s in range(OWN):

            def pick(q, s=s):
                ref, i = dlow.at(q)
                return ref[i, HID * s : HID * s + HID, :]

            p = dot(wgear[...], taps((r + 2, r + 1, r), pick))
            for d in range(2):
                ref, i = low.at(r + d)
                ref[i, s] = gather_columns(p[:, COLS * d : COLS * d + COLS]).astype(BF16)


def grad_rows(ig3, rg3):
    rows = Rows(ig3, rg3, FLD_INNER)

    def pick(s, r):
        ref, i = rows.at(r)
        return ref[s, i]

    return pick


def feature_grad_stage(dref, jobs, unroll):
    def step(i, carry):
        r = 2 * i
        for first, size, weight, out, s in jobs:
            rhs = taps((r + 2, r + 1, r), lambda q: dref[q, first : first + size, :])
            p = dot(weight[...], rhs)
            for d in range(2):
                out[r + d, s] = gather_columns(p[:, COLS * d : COLS * d + COLS]).astype(out.dtype)
        return carry

    lax.fori_loop(0, TR // 2, step, 0, unroll=unroll)


def borrowed_kernel(
    psib, pouter, xp, rcur, rtown, itsum, ihmid, ig3, idlow, rcot, consts,
    wear, w2first, w2rest, w2b, w2brest, wgear,
    low, rhmid, rg3, rvotes,
    wide, xr, rtsum, fld, grd, rdlow,
):
    odd = odd_tile()
    has = has_tiles()
    keep = (lax.axis_index("sec") > 0).astype(F32)
    for s in range(OWN):
        wide[s] = psib[s].astype(F32)

    def halo(side, s, r):
        at = (r * OWN + s) * CH
        y = pouter[at : at + CH, :].astype(F32)
        if side == 0:
            return jnp.where(odd, wide[s, :, TR - HALO + r, :], y)
        return jnp.where(odd, y, wide[s, :, r, :])

    spread_rim(halo, [keep * h for h in has], xr)
    hmid, tsum = Rows(ihmid, rhmid), Rows(itsum, rtsum)
    hidden_borrowed(
        RIM_PAIRS, feature_rows(xp, xr), wear, w2first, w2rest,
        Rows(None, rcur), Rows(None, rtown), hmid, tsum,
    )
    fields_stage(rim_rows(FLD_INNER), tsum, consts.at[OWN], has, fld)
    vote_stage(2 * HALO, consts, lambda s, c: rcot[s, c], fld, grd, rg3, rvotes)
    dlow = Rows(idlow, rdlow, DH_INNER)
    low_grad_stage(rim_rows(DH_INNER, 2), w2b, w2brest, grad_rows(ig3, rg3), hmid, dlow)
    inside(rdlow, has)
    low_stage(rim_rows(OUT_INNER, 2), wgear, dlow, Rows(None, low, OUT_INNER))


def borrowed(*args):
    return call(
        borrowed_kernel,
        [
            ((2 * HALO, OWN, CH, COLS), BF16),
            ((RIM, 6 * HID, COLS), BF16),
            ((OWN, 2 * HALO, 32, COLS), BF16),
            ((OWN, 2, 8, COLS), F32),
        ],
        [
            ((OWN, CH, TR, COLS), F32),
            ((OWN, 2 * HALO, 3 * CH, COLS), BF16),
            ((RIM, OWN * 72, COLS), F32),
            ((OWN, 2 * HALO, 8, COLS), F32),
            ((OWN, 2 * HALO, 8, COLS), F32),
            ((2 * HALO, 3 * HID, COLS), BF16),
        ],
        6,
        "borrowed",
        "v" * len(args),
        *args,
    )


def own_grad_kernel(
    ivotes, rvotes, ig3, rg3, ihown, rhown, ihmid, rhmid, w2b, wgcur, wgboth, voted, grad, down
):
    has = has_tiles()
    hown, hmid = Rows(ihown, rhown), Rows(ihmid, rhmid)
    g3 = grad_rows(ig3, rg3)
    for s in range(OWN):
        for c in range(2):
            voted[s, c, 0:2, :] = rvotes[s, c, 2:4, :]
            voted[s, c, 2 : TR - 2, :] = ivotes[s, c, 0:FLD_INNER, :]
            voted[s, c, TR - 2 :, :] = rvotes[s, c, 4:6, :]
    for q in range(0, DH_ROWS, 2):
        ho = hown.pair(q + 2, 0, 192)
        hm = hmid.pair(q + 2, 0, 384)
        h = [
            hm[:192],
            jnp.concatenate([ho[:64], hm[192:320]], axis=0),
            jnp.concatenate([ho[64:], hm[320:]], axis=0),
        ]
        m = []
        for s in range(OWN):
            dh = dot(w2b[...], taps((q + 2, q + 1, q), lambda r, s=s: g3(s, r)))
            dh = jnp.where(h[s].astype(F32) > 0.0, dh, 0.0)
            m.append([dh[HID * k : HID * k + HID] for k in range(3)])
        c = [m[s][0] + m[s][1] + m[s][2] for s in range(OWN)]
        d = jnp.concatenate([c[0], m[1][0] + m[2][1], c[1], m[2][0], c[2]], axis=0).astype(BF16)
        halves(down, q, 0, d)
    inside(down, has)
    feature_grad_stage(
        down,
        [(0, 128, wgboth, grad, 0), (128, 128, wgboth, grad, 1), (256, 64, wgcur, grad, 2)],
        4,
    )


def own_grad(*args):
    return call(
        own_grad_kernel,
        [((OWN, 2, TR, COLS), F32), ((TR, OWN, CH, COLS), F32)],
        [((DH_ROWS, 5 * HID, COLS), BF16)],
        4,
        "own_grad",
        "v" * len(args),
        *args,
    )


def finish_kernel(grad, iback, rback, out, block, sems):
    keep = (lax.axis_index("sec") < lax.axis_size("sec") - 1).astype(F32)
    back = Rows(iback, rback, OUT_INNER)
    copies = []
    for s in range(OWN):
        for r in range(TR):
            ref, i = back.at(r)
            block[s, :, r, :] = grad[r, s] + ref[i, s].astype(F32) * keep
        copies.append(pltpu.make_async_copy(block.at[s], out.at[s], sems.at[s]))
        copies[-1].start()
    for c in copies:
        c.wait()


def finish(*args):
    vmem = pl.BlockSpec(memory_space=pltpu.VMEM)
    return pl.pallas_call(
        finish_kernel,
        out_shape=jax.ShapeDtypeStruct((OWN, CH, TR, COLS), F32),
        in_specs=[vmem] * len(args),
        out_specs=pl.BlockSpec(memory_space=pltpu.HBM),
        scratch_shapes=[
            pltpu.VMEM((OWN, CH, TR, COLS), F32),
            pltpu.SemaphoreType.DMA((OWN,)),
        ],
        compiler_params=params(2),
        name="finish",
    )(*args)


def move(value, secs, tile_to, wrap=True):
    n, m = lax.axis_size("sec"), lax.axis_size("tile")
    pairs = []
    for a in range(n):
        for b in range(m):
            to = tile_to(b)
            if wrap:
                pairs.append((a * m + b, a * m + b if to is None else ((a + secs) % n) * m + to))
            elif to is not None and 0 <= a + secs < n:
                pairs.append((a * m + b, (a + secs) * m + to))
    return lax.ppermute(value, ("sec", "tile"), pairs)


def body(
    features, vote_grad, sharpness, valid_rows, first_kernel, first_bias, second_kernel, second_bias
):
    tiles = lax.axis_size("tile")

    def same(b):
        return b

    def to_sibling(b):
        return b + 1 - 2 * (b % 2)

    def to_outer(b):
        other = b - 1 + 2 * (b % 2)
        return other if 0 <= other < tiles else None

    prev = move(features, 1, same)
    for_sibling, for_outer, wide, cot16, consts, k1, k2, b1 = edges(
        valid_rows, sharpness, second_bias, features, vote_grad,
        first_kernel, second_kernel, first_bias[None],
    )
    sibling = move(for_sibling, 0, to_sibling)
    outer = move(for_outer, 0, to_outer)
    pouter = move(for_outer, 1, to_outer, False)
    (
        wcur, wear, wboth, w2own, w2first, w2rest, w2b, w2brest, wgear, wgcur, wgboth, bias,
    ) = weights(k1, k2, b1)
    xd, icur, ihown, itown = own_inner(wide, wcur, wboth, bias, w2own)
    rcur, rhown, rtown, rcot = own_rim(
        sibling, outer, cot16, xd, wcur, wboth, bias, w2own
    )
    prev, rcur, pouter = lax.optimization_barrier((prev, rcur, pouter))
    psib = move(prev, 0, to_sibling)
    ilow, xp, ihmid, itsum, ig3, ivotes, idlow = middle(
        prev, icur, itown, cot16, consts, wear, w2first, w2rest, w2b, w2brest, wgear
    )
    iback = move(ilow, -1, same)
    rlow, rhmid, rg3, rvotes = borrowed(
        psib, pouter, xp, rcur, rtown, itsum, ihmid, ig3, idlow, rcot, consts,
        wear, w2first, w2rest, w2b, w2brest, wgear,
    )
    rback = move(rlow, -1, same)
    voted, grad = own_grad(
        ivotes, rvotes, ig3, rg3, ihown, rhown, ihmid, rhmid, w2b, wgcur, wgboth
    )
    return (voted, finish(grad, iback, rback))


def solution(mesh):
    return jax.shard_map(
        body,
        mesh=mesh,
        in_specs=(
            P("sec", None, "tile", None),
            P("sec", None, "tile", None),
            P("sec"),
            P("sec"),
            P(),
            P(),
            P(),
            P(),
        ),
        out_specs=(P("sec", None, "tile", None), P("sec", None, "tile", None)),
        check_vma=False,
    )
```

```python
import jax
import jax.numpy as jnp
from jax import lax
from jax.experimental import pallas as pl
from jax.experimental.pallas import tpu as pltpu
from jax.sharding import PartitionSpec as P

F32 = jnp.float32
BF16 = jnp.bfloat16
OWN = 3
CH = 32
HID = 64
TR = 16
COLS = 128
HALO = 4
FEAT_ROWS = TR + 2 * HALO
HID_ROWS = FEAT_ROWS - 2
FLD_ROWS = FEAT_ROWS - 4
DH_ROWS = FEAT_ROWS - 6
EDGE = HALO * OWN * CH
EDGE_ALL = EDGE + 32


def lane(shape):
    return lax.broadcasted_iota(jnp.int32, shape, len(shape) - 1)


def from_left(x):
    return jnp.where(lane(x.shape) == 0, 0.0, pltpu.roll(x, 1, x.ndim - 1))


def from_right(x):
    return jnp.where(lane(x.shape) == COLS - 1, 0.0, pltpu.roll(x, COLS - 1, x.ndim - 1))


def dot(a, b):
    return jnp.dot(a, b, preferred_element_type=F32)


def params(mib):
    return pltpu.CompilerParams(vmem_limit_bytes=mib << 20)


COST = {
    "own_rim": 0,
    "edges": 0,
    "weights": 0,
    "own_inner": 0,
    "middle": 2306,
    "borrowed": 3459,
    "own_grad": 3459,
    "finish": 1153,
}
INNER = TR - 2
RIM = HID_ROWS - INNER
INNER_PAIRS = [HALO + 2 * i for i in range(INNER // 2)]
RIM_PAIRS = [0, 2, HALO + INNER, HALO + INNER + 2]
FLD_INNER = FLD_ROWS - 2 * HALO
DH_INNER = DH_ROWS - 2 * HALO
OUT_INNER = TR - 2 * HALO


def inner_rows(count, step=1):
    return range(HALO, HALO + count, step)


def rim_rows(count, step=1):
    return [*range(0, HALO, step), *range(HALO + count, 2 * HALO + count, step)]


def call(kernel, outs, scratch, mib, name, specs, *args):
    space = {"v": pltpu.VMEM, "h": pltpu.HBM}
    args = [
        pltpu.with_memory_space_constraint(x, pltpu.HBM) if c == "h" else x
        for x, c in zip(args, specs, strict=True)
    ]
    return pl.pallas_call(
        kernel,
        out_shape=tuple(jax.ShapeDtypeStruct(shape, kind) for shape, kind in outs),
        in_specs=[pl.BlockSpec(memory_space=space[c]) for c in specs],
        out_specs=(pl.BlockSpec(memory_space=pltpu.VMEM),) * len(outs),
        scratch_shapes=[
            item[0](item[1], item[2]) if len(item) == 3 else pltpu.VMEM(*item) for item in scratch
        ],
        compiler_params=params(mib),
        cost_estimate=pl.CostEstimate(
            flops=COST[name] * 10**6, bytes_accessed=0, transcendentals=0
        ),
        name=name,
    )(*args)


def sems(shape, _):
    return pltpu.SemaphoreType.DMA(shape)


def fetch(sems, *moves):
    copies = [pltpu.make_async_copy(a, b, sems.at[i]) for i, (a, b) in enumerate(moves)]
    for c in copies:
        c.start()
    for c in copies:
        c.wait()


def odd_tile():
    return lax.axis_index("tile") % 2 == 1


def has_tiles():
    tile = lax.axis_index("tile")
    return (tile > 0).astype(F32), (tile < lax.axis_size("tile") - 1).astype(F32)


class Rows:
    def __init__(self, inner, rim, count=INNER):
        self.inner, self.rim, self.count = inner, rim, count

    def at(self, r):
        if r < HALO:
            return self.rim, r
        if r < HALO + self.count:
            return self.inner, r - HALO
        return self.rim, r - self.count

    def pair(self, r, first, n):
        ref, i = self.at(r)
        return pair_row(ref, i, first, n)

    def put(self, r, first, x):
        ref, i = self.at(r)
        halves(ref, i, first, x)


def edges_kernel(
    valid_hbm, sharp_hbm, b2_hbm, feat_hbm, vgrad_hbm,
    sibling, outer, wide, cot, consts,
    valid, sharp, b2, feat, vgrad, ext, sems,
):
    fetch(
        sems,
        (feat_hbm, feat), (vgrad_hbm, vgrad), (valid_hbm, valid), (sharp_hbm, sharp), (b2_hbm, b2),
    )
    row0 = lax.axis_index("tile") * TR
    odd = odd_tile()
    for s in range(OWN):
        wide[s] = feat[s].astype(F32)
        pos = row0 + lax.broadcasted_iota(jnp.int32, (TR, COLS), 0)
        for c in range(2):
            cot[s, c] = jnp.where(pos < valid[s], vgrad[s, c], 0.0)
        consts[s] = jnp.full((8, COLS), sharp[s], F32)
    even_row = lax.broadcasted_iota(jnp.int32, (8, COLS), 0) % 2 == 0
    consts[OWN] = jnp.where(even_row, b2[0], b2[1])
    for out, last in ((sibling, jnp.logical_not(odd)), (outer, odd)):
        ext[...] = jnp.zeros((32, COLS), F32)
        for s in range(OWN):
            for c in range(2):
                x = jnp.where(last, cot[s, c, TR - 2 :, :], cot[s, c, 0:2, :])
                high = x.astype(BF16).astype(F32)
                at = s * 4 + c * 2
                ext[at : at + 2, :] = high
                ext[12 + at : 14 + at, :] = x - high
        out[EDGE:, :] = ext[...].astype(BF16)
        for s in range(OWN):
            for r in range(HALO):
                at = (r * OWN + s) * CH
                x = jnp.where(last, wide[s, :, TR - HALO + r, :], wide[s, :, r, :])
                out[at : at + CH, :] = x.astype(BF16)


def edges(*args):
    return call(
        edges_kernel,
        [
            ((EDGE_ALL, COLS), BF16),
            ((EDGE_ALL, COLS), BF16),
            ((OWN, CH, TR, COLS), F32),
            ((OWN, 2, TR, COLS), F32),
            ((OWN + 1, 8, COLS), F32),
        ],
        [
            (pltpu.SMEM, (OWN,), jnp.int32),
            (pltpu.SMEM, (OWN,), F32),
            (pltpu.SMEM, (2,), F32),
            ((OWN, CH, TR, COLS), BF16),
            ((OWN, 2, TR, COLS), F32),
            ((32, COLS), F32),
            (sems, (5,), None),
        ],
        3,
        "edges",
        "hhhhh",
        *args,
    )


def weights_kernel(
    k1_hbm, k2_hbm, b1_hbm, wcur, wear, wboth, w2own, w2first, w2rest, w2b, w2brest, wgear, wgcur, wgboth, bias,
    k1, k2, b1, fwd, bwd, both, two, sq, sems,
):
    fetch(sems, (k1_hbm, k1), (k2_hbm, k2), (b1_hbm, b1))
    bias[...] = jnp.broadcast_to(b1[...], (COLS, HID)).T
    for dy in range(3):
        for dx in range(3):
            k = k1[dy, dx].astype(F32)
            t = CH * (3 * dy + dx)
            fwd[0:HID, t : t + CH] = k[:, :CH]
            fwd[HID:, t : t + CH] = k[:, CH:]
            kt = k.T
            rows = slice(CH * dx, CH * dx + CH)
            bwd[rows, HID * dy : HID * dy + HID] = kt[:CH]
            bwd[3 * CH + CH * dx : 4 * CH + CH * dx, HID * dy : HID * dy + HID] = kt[CH:]
            both[rows, 2 * HID * dy : 2 * HID * dy + HID] = kt[:CH]
            both[rows, 2 * HID * dy + HID : 2 * HID * dy + 2 * HID] = kt[CH:]
    wcur[...] = fwd[0:HID, :].astype(BF16)
    wear[...] = fwd[HID:, :].astype(BF16)
    wboth[...] = fwd[...].astype(BF16)
    wgcur[...] = bwd[0 : 3 * CH, :].astype(BF16)
    wgear[...] = bwd[3 * CH :, :].astype(BF16)
    wgboth[...] = both[...].astype(BF16)

    def put(ref, row, col, lags):
        for i, lag in enumerate(lags):
            for dy in range(3):
                for dx in range(3):
                    at = row + 8 * (3 * dy + dx) + 2 * lag
                    c = col + HID * i
                    ref[at : at + 2, c : c + HID] = k2[dy, dx].astype(F32)

    two[...] = jnp.zeros(two.shape, F32)
    put(two, 0, 0, (0, 1, 2))
    w2first[...] = two[0:72, :].astype(BF16)
    two[...] = jnp.zeros(two.shape, F32)
    put(two, 0, 0, (1, 2))
    put(two, 72, 2 * HID, (2,))
    w2rest[...] = two[...].astype(BF16)
    two[...] = jnp.zeros(two.shape, F32)
    put(two, 0, 0, (0,))
    put(two, 72, HID, (0, 1))
    w2own[...] = two[...].astype(BF16)

    def lay(row, col, lags):
        for i, lag in enumerate(lags):
            for dy in range(3):
                for dx in range(3):
                    at = row + 32 * dy + 8 * dx + 2 * lag
                    c = col + HID * i
                    sq[at : at + 2, c : c + HID] = k2[dy, dx].astype(F32)

    sq[...] = jnp.zeros(sq.shape, F32)
    lay(0, 0, (0, 1, 2))
    w2b[...] = sq[0:96, :].T.astype(BF16)
    sq[...] = jnp.zeros(sq.shape, F32)
    lay(0, 0, (1, 2))
    lay(96, 2 * HID, (2,))
    w2brest[...] = sq[...].T.astype(BF16)


def weights(k1, k2, b1):
    return call(
        weights_kernel,
        [
            ((HID, 9 * CH), BF16),
            ((HID, 9 * CH), BF16),
            ((2 * HID, 9 * CH), BF16),
            ((144, 192), BF16),
            ((72, 192), BF16),
            ((144, 192), BF16),
            ((192, 96), BF16),
            ((192, 192), BF16),
            ((3 * CH, 3 * HID), BF16),
            ((3 * CH, 3 * HID), BF16),
            ((3 * CH, 6 * HID), BF16),
            ((HID, COLS), F32),
        ],
        [
            (k1.shape, BF16),
            (k2.shape, BF16),
            (b1.shape, F32),
            ((2 * HID, 9 * CH), F32),
            ((6 * CH, 3 * HID), F32),
            ((3 * CH, 6 * HID), F32),
            ((144, 192), F32),
            ((192, 192), F32),
            (sems, (3,), None),
        ],
        4,
        "weights",
        "hhh",
        k1,
        k2,
        b1,
    )


def spread_row(x, xd, j, r):
    xd[j, r, 0:CH, :] = from_left(x).astype(BF16)
    xd[j, r, CH : 2 * CH, :] = x.astype(BF16)
    xd[j, r, 2 * CH :, :] = from_right(x).astype(BF16)


def spread_own(wide, keep, xd):
    for s in range(OWN):
        for r in range(TR):
            x = wide[s, :, r, :]
            spread_row(x if keep is None else x * keep, xd, s, r)


def spread_rim(pick, scale, xr):
    for s in range(OWN):
        for r in range(HALO):
            for side in range(2):
                spread_row(pick(side, s, r) * scale[side], xr, s, HALO * side + r)


def feature_rows(xd, xr):
    def pick(j, r):
        if r < HALO:
            return xr[j, r]
        if r < HALO + TR:
            return xd[j, r - HALO]
        return xr[j, r - TR]

    return pick


def taps(rows, pick):
    return jnp.concatenate(
        [jnp.concatenate([pick(r), pick(r + 1)], axis=1) for r in rows], axis=0
    )


def halves(ref, r, first, x):
    n = x.shape[0]
    ref[r, first : first + n, :] = x[:, :COLS]
    ref[r + 1, first : first + n, :] = x[:, COLS:]


def pair_row(ref, r, first, n):
    return jnp.concatenate(
        [ref[r, first : first + n, :], ref[r + 1, first : first + n, :]], axis=1
    )


def gather_columns(p):
    return from_right(p[:CH]) + p[CH : 2 * CH] + from_left(p[2 * CH :])


def hidden_own(pairs, pick, wcur, wboth, bias, w2own, cur, hown, town):
    b = jnp.concatenate([bias[...], bias[...]], axis=1)
    for r in pairs:
        rhs = [taps((r, r + 1, r + 2), lambda q, j=j: pick(j, q)) for j in range(OWN)]
        both = [dot(wboth[...], rhs[j]) for j in range(2)]
        c = [both[0][:HID] + b, both[1][:HID] + b, dot(wcur[...], rhs[2]) + b]
        ear = [both[0][HID:], both[1][HID:]]
        for s in range(OWN):
            cur.put(r, HID * s, c[s])
        h = jnp.concatenate(
            [jnp.maximum(x, 0.0) for x in (c[1] + ear[0], c[2] + ear[1], c[2] + ear[0])], axis=0
        ).astype(BF16)
        hown.put(r, 0, h)
        town.put(r, 0, dot(w2own[...], h))


def hidden_borrowed(pairs, pick, wear, w2first, w2rest, cur, town, hmid, tsum):
    for r in pairs:
        ear = [
            dot(wear[...], taps((r, r + 1, r + 2), lambda q, j=j: pick(j, q)))
            for j in range(OWN)
        ]
        c = [cur.pair(r, HID * s, HID) for s in range(OWN)]
        h = [
            jnp.concatenate([jnp.maximum(c[s] + ear[3 + s - k], 0.0) for s, k in part], axis=0)
            for part in (((0, 1), (0, 2), (0, 3)), ((1, 2), (1, 3), (2, 3)))
        ]
        h = [x.astype(BF16) for x in h]
        hmid.put(r, 0, h[0])
        hmid.put(r, 192, h[1])
        tsum.put(r, 0, dot(w2first[...], h[0]))
        tsum.put(r, 72, dot(w2rest[...], h[1]) + town.pair(r, 0, 144))


def own_kernel(wide, wcur, wboth, bias, w2own, xd, cur, hown, town):
    spread_own(wide, None, xd)
    hidden_own(
        INNER_PAIRS, feature_rows(xd, None), wcur, wboth, bias, w2own,
        Rows(cur, None), Rows(hown, None), Rows(town, None),
    )


def hidden_outs(n):
    return [
        ((n, OWN * HID, COLS), F32),
        ((n, 3 * HID, COLS), BF16),
        ((n, 144, COLS), F32),
    ]


def own_inner(*args):
    return call(
        own_kernel,
        [((OWN, TR, 3 * CH, COLS), BF16)] + hidden_outs(INNER),
        [],
        2,
        "own_inner",
        "v" * len(args),
        *args,
    )


def rim_kernel(
    sibling, outer, cot16, xd, wcur, wboth, bias, w2own, rcur, rhown, rtown, rcot, xr
):
    odd = odd_tile()
    has = has_tiles()

    def halo(side, first, n):
        x, y = sibling[first : first + n, :], outer[first : first + n, :]
        x, y = x.astype(F32), y.astype(F32)
        return jnp.where(odd, x, y) if side == 0 else jnp.where(odd, y, x)

    for side, first in ((0, 0), (1, 6)):
        ext = halo(side, EDGE, 32) * has[side]
        for s in range(OWN):
            for c in range(2):
                at = s * 4 + c * 2
                rcot[s, c, first : first + 2, :] = ext[at : at + 2] + ext[12 + at : 14 + at]
    for s in range(OWN):
        for c in range(2):
            rcot[s, c, 2:4, :] = cot16[s, c, 0:2, :]
            rcot[s, c, 4:6, :] = cot16[s, c, TR - 2 :, :]
    spread_rim(lambda side, s, r: halo(side, (r * OWN + s) * CH, CH), has, xr)
    hidden_own(
        RIM_PAIRS, feature_rows(xd, xr), wcur, wboth, bias, w2own,
        Rows(None, rcur), Rows(None, rhown), Rows(None, rtown),
    )


def own_rim(*args):
    return call(
        rim_kernel,
        hidden_outs(RIM) + [((OWN, 2, 8, COLS), F32)],
        [((OWN, 2 * HALO, 3 * CH, COLS), BF16)],
        2,
        "own_rim",
        "v" * len(args),
        *args,
    )


def middle_kernel(
    prev, icur, itown, cot16, consts, wear, w2first, w2rest, w2b, w2brest, wgear,
    low, xp, ihmid, itsum, ig3, ivotes, idlow,
    wide, fld, grd,
):
    keep = (lax.axis_index("sec") > 0).astype(F32)
    for s in range(OWN):
        wide[s] = prev[s].astype(F32)
    spread_own(wide, keep, xp)
    hmid, tsum = Rows(ihmid, None), Rows(itsum, None)
    hidden_borrowed(
        INNER_PAIRS, feature_rows(xp, None), wear, w2first, w2rest,
        Rows(icur, None), Rows(itown, None), hmid, tsum,
    )
    fields_stage(inner_rows(FLD_INNER), tsum, consts.at[OWN], None, fld)
    vote_stage(
        FLD_INNER, consts, lambda s, c: cot16[s, c, 2 : TR - 2, :], fld, grd, ig3, ivotes
    )
    dlow = Rows(idlow, None, DH_INNER)
    low_grad_stage(
        inner_rows(DH_INNER, 2), w2b, w2brest, grad_rows(ig3, None), hmid, dlow
    )
    low_stage(inner_rows(OUT_INNER, 2), wgear, dlow, Rows(low, None, OUT_INNER))


def middle(*args):
    return call(
        middle_kernel,
        [
            ((OUT_INNER, OWN, CH, COLS), BF16),
            ((OWN, TR, 3 * CH, COLS), BF16),
            ((INNER, 6 * HID, COLS), BF16),
            ((INNER, OWN * 72, COLS), F32),
            ((OWN, FLD_INNER, 32, COLS), BF16),
            ((OWN, 2, 16, COLS), F32),
            ((DH_INNER, 3 * HID, COLS), BF16),
        ],
        [
            ((OWN, CH, TR, COLS), F32),
            ((OWN, FLD_INNER, 8, COLS), F32),
            ((OWN, FLD_INNER, 8, COLS), F32),
        ],
        4,
        "middle",
        "v" * len(args),
        *args,
    )


def fields_stage(rows, tsum, bias2, has, fld):
    for i, r in enumerate(rows):
        for s in range(OWN):
            sums = []
            for dx in range(3):
                terms = []
                for dy in range(3):
                    at = 72 * s + 8 * (3 * dy + dx)
                    ref, j = tsum.at(r + dy)
                    t = ref[j, at : at + 8, :]
                    if r + dy < 3:
                        t = t * has[0]
                    elif r + dy > HID_ROWS - 4:
                        t = t * has[1]
                    terms.append(t)
                sums.append(terms[0] + terms[1] + terms[2])
            fld[s, i] = (sums[1] + bias2[...]) + (from_left(sums[0]) + from_right(sums[2]))


def vote_stage(n, consts, cot_of, fld, grd, g3, votes):
    for s in range(OWN):
        f = [[fld[s, :, 2 * k + c, :] for c in range(2)] for k in range(3)]
        beta = consts[s, 0:1, :]
        diff = {}
        dist = {}
        for a, b in ((0, 1), (0, 2), (1, 2)):
            diff[a, b] = [f[a][c] - f[b][c] for c in range(2)]
            dist[a, b] = diff[a, b][0] * diff[a, b][0] + diff[a, b][1] * diff[a, b][1]
        score = [dist[0, 1] + dist[0, 2], dist[0, 1] + dist[1, 2], dist[0, 2] + dist[1, 2]]
        logit = [-beta * q for q in score]
        top = jnp.maximum(jnp.maximum(logit[0], logit[1]), logit[2])
        expo = [jnp.exp(q - top) for q in logit]
        inv = 1.0 / (expo[0] + expo[1] + expo[2])
        w = [q * inv for q in expo]
        v = [w[0] * f[0][c] + w[1] * f[1][c] + w[2] * f[2][c] for c in range(2)]
        for c in range(2):
            votes[s, c, 0:n, :] = v[c]
        g = [cot_of(s, c) for c in range(2)]
        e = [
            -beta * w[k] * (g[0] * (f[k][0] - v[0]) + g[1] * (f[k][1] - v[1])) for k in range(3)
        ]
        pair = {key: 2.0 * (e[key[0]] + e[key[1]]) for key in diff}
        for c in range(2):
            m01 = pair[0, 1] * diff[0, 1][c]
            m02 = pair[0, 2] * diff[0, 2][c]
            m12 = pair[1, 2] * diff[1, 2][c]
            grd[s, :, 0 + c, :] = w[0] * g[c] + m01 + m02
            grd[s, :, 2 + c, :] = w[1] * g[c] - m01 + m12
            grd[s, :, 4 + c, :] = w[2] * g[c] - m02 - m12
        grd[s, :, 6, :] = jnp.zeros((n, COLS), F32)
        grd[s, :, 7, :] = jnp.zeros((n, COLS), F32)
    for r in range(n):
        for s in range(OWN):
            x = grd[s, r]
            g3[s, r] = jnp.concatenate(
                [from_right(x), x, from_left(x), jnp.zeros_like(x)], axis=0
            ).astype(BF16)


def inside(ref, has):
    for r, h in ((0, has[0]), (ref.shape[0] - 1, has[1])):
        ref[r] = (ref[r].astype(F32) * h).astype(BF16)


def low_grad_stage(rows, w2b, w2brest, g3, hmid, dlow):
    for q in rows:
        rhs = [taps((q + 2, q + 1, q), lambda r, s=s: g3(s, r)) for s in range(OWN)]
        h = [hmid.pair(q + 2, 192 * j, 192).astype(F32) for j in range(2)]
        first = jnp.where(h[0] > 0.0, dot(w2b[...], rhs[0]), 0.0)
        rest = jnp.where(
            h[1] > 0.0, dot(w2brest[...], jnp.concatenate([rhs[1], rhs[2]], axis=0)), 0.0
        )
        low = jnp.concatenate(
            [
                first[2 * HID :],
                first[HID : 2 * HID] + rest[HID : 2 * HID],
                first[:HID] + rest[:HID] + rest[2 * HID :],
            ],
            axis=0,
        ).astype(BF16)
        dlow.put(q, 0, low)


def low_stage(rows, wgear, dlow, low):
    for r in rows:
        for s in range(OWN):

            def pick(q, s=s):
                ref, i = dlow.at(q)
                return ref[i, HID * s : HID * s + HID, :]

            p = dot(wgear[...], taps((r + 2, r + 1, r), pick))
            for d in range(2):
                ref, i = low.at(r + d)
                ref[i, s] = gather_columns(p[:, COLS * d : COLS * d + COLS]).astype(BF16)


def grad_rows(ig3, rg3):
    rows = Rows(ig3, rg3, FLD_INNER)

    def pick(s, r):
        ref, i = rows.at(r)
        return ref[s, i]

    return pick


def feature_grad_stage(dref, jobs, unroll):
    def step(i, carry):
        r = 2 * i
        for first, size, weight, out, s in jobs:
            rhs = taps((r + 2, r + 1, r), lambda q: dref[q, first : first + size, :])
            p = dot(weight[...], rhs)
            for d in range(2):
                out[r + d, s] = gather_columns(p[:, COLS * d : COLS * d + COLS]).astype(out.dtype)
        return carry

    lax.fori_loop(0, TR // 2, step, 0, unroll=unroll)


def borrowed_kernel(
    psib, pouter, xp, rcur, rtown, itsum, ihmid, ig3, idlow, rcot, consts,
    wear, w2first, w2rest, w2b, w2brest, wgear,
    low, rhmid, rg3, rvotes,
    wide, xr, rtsum, fld, grd, rdlow,
):
    odd = odd_tile()
    has = has_tiles()
    keep = (lax.axis_index("sec") > 0).astype(F32)
    for s in range(OWN):
        wide[s] = psib[s].astype(F32)

    def halo(side, s, r):
        at = (r * OWN + s) * CH
        y = pouter[at : at + CH, :].astype(F32)
        if side == 0:
            return jnp.where(odd, wide[s, :, TR - HALO + r, :], y)
        return jnp.where(odd, y, wide[s, :, r, :])

    spread_rim(halo, [keep * h for h in has], xr)
    hmid, tsum = Rows(ihmid, rhmid), Rows(itsum, rtsum)
    hidden_borrowed(
        RIM_PAIRS, feature_rows(xp, xr), wear, w2first, w2rest,
        Rows(None, rcur), Rows(None, rtown), hmid, tsum,
    )
    fields_stage(rim_rows(FLD_INNER), tsum, consts.at[OWN], has, fld)
    vote_stage(2 * HALO, consts, lambda s, c: rcot[s, c], fld, grd, rg3, rvotes)
    dlow = Rows(idlow, rdlow, DH_INNER)
    low_grad_stage(rim_rows(DH_INNER, 2), w2b, w2brest, grad_rows(ig3, rg3), hmid, dlow)
    inside(rdlow, has)
    low_stage(rim_rows(OUT_INNER, 2), wgear, dlow, Rows(None, low, OUT_INNER))


def borrowed(*args):
    return call(
        borrowed_kernel,
        [
            ((2 * HALO, OWN, CH, COLS), BF16),
            ((RIM, 6 * HID, COLS), BF16),
            ((OWN, 2 * HALO, 32, COLS), BF16),
            ((OWN, 2, 8, COLS), F32),
        ],
        [
            ((OWN, CH, TR, COLS), F32),
            ((OWN, 2 * HALO, 3 * CH, COLS), BF16),
            ((RIM, OWN * 72, COLS), F32),
            ((OWN, 2 * HALO, 8, COLS), F32),
            ((OWN, 2 * HALO, 8, COLS), F32),
            ((2 * HALO, 3 * HID, COLS), BF16),
        ],
        6,
        "borrowed",
        "v" * len(args),
        *args,
    )


def own_grad_kernel(
    ivotes, rvotes, ig3, rg3, ihown, rhown, ihmid, rhmid, w2b, wgcur, wgboth, voted, grad, down
):
    has = has_tiles()
    hown, hmid = Rows(ihown, rhown), Rows(ihmid, rhmid)
    g3 = grad_rows(ig3, rg3)
    for s in range(OWN):
        for c in range(2):
            voted[s, c, 0:2, :] = rvotes[s, c, 2:4, :]
            voted[s, c, 2 : TR - 2, :] = ivotes[s, c, 0:FLD_INNER, :]
            voted[s, c, TR - 2 :, :] = rvotes[s, c, 4:6, :]
    for q in range(0, DH_ROWS, 2):
        ho = hown.pair(q + 2, 0, 192)
        hm = hmid.pair(q + 2, 0, 384)
        h = [
            hm[:192],
            jnp.concatenate([ho[:64], hm[192:320]], axis=0),
            jnp.concatenate([ho[64:], hm[320:]], axis=0),
        ]
        m = []
        for s in range(OWN):
            dh = dot(w2b[...], taps((q + 2, q + 1, q), lambda r, s=s: g3(s, r)))
            dh = jnp.where(h[s].astype(F32) > 0.0, dh, 0.0)
            m.append([dh[HID * k : HID * k + HID] for k in range(3)])
        c = [m[s][0] + m[s][1] + m[s][2] for s in range(OWN)]
        d = jnp.concatenate([c[0], m[1][0] + m[2][1], c[1], m[2][0], c[2]], axis=0).astype(BF16)
        halves(down, q, 0, d)
    inside(down, has)
    feature_grad_stage(
        down,
        [(0, 128, wgboth, grad, 0), (128, 128, wgboth, grad, 1), (256, 64, wgcur, grad, 2)],
        4,
    )


def own_grad(*args):
    return call(
        own_grad_kernel,
        [((OWN, 2, TR, COLS), F32), ((TR, OWN, CH, COLS), F32)],
        [((DH_ROWS, 5 * HID, COLS), BF16)],
        4,
        "own_grad",
        "v" * len(args),
        *args,
    )


def finish_kernel(grad, iback, rback, out, block, sems):
    keep = (lax.axis_index("sec") < lax.axis_size("sec") - 1).astype(F32)
    back = Rows(iback, rback, OUT_INNER)
    copies = []
    part = CH // 2
    for s in range(OWN):
        for half in range(2):
            at = slice(part * half, part * half + part)
            for r in range(TR):
                ref, i = back.at(r)
                block[s, at, r, :] = grad[r, s, at, :] + ref[i, s, at, :].astype(F32) * keep
            copies.append(
                pltpu.make_async_copy(block.at[s, at], out.at[s, at], sems.at[2 * s + half])
            )
            copies[-1].start()
    for c in copies:
        c.wait()


def finish(*args):
    vmem = pl.BlockSpec(memory_space=pltpu.VMEM)
    return pl.pallas_call(
        finish_kernel,
        out_shape=jax.ShapeDtypeStruct((OWN, CH, TR, COLS), F32),
        in_specs=[vmem] * len(args),
        out_specs=pl.BlockSpec(memory_space=pltpu.HBM),
        scratch_shapes=[
            pltpu.VMEM((OWN, CH, TR, COLS), F32),
            pltpu.SemaphoreType.DMA((2 * OWN,)),
        ],
        compiler_params=params(2),
        name="finish",
    )(*args)


def move(value, secs, tile_to):
    n, m = lax.axis_size("sec"), lax.axis_size("tile")
    pairs = []
    for a in range(n):
        for b in range(m):
            to = tile_to(b)
            pairs.append((a * m + b, a * m + b if to is None else ((a + secs) % n) * m + to))
    return lax.ppermute(value, ("sec", "tile"), pairs)


def body(
    features, vote_grad, sharpness, valid_rows, first_kernel, first_bias, second_kernel, second_bias
):
    tiles = lax.axis_size("tile")

    def same(b):
        return b

    def to_sibling(b):
        return b + 1 - 2 * (b % 2)

    def to_outer(b):
        other = b - 1 + 2 * (b % 2)
        return other if 0 <= other < tiles else None

    prev = move(features, 1, same)
    for_sibling, for_outer, wide, cot16, consts = edges(
        valid_rows, sharpness, second_bias, features, vote_grad
    )
    sibling = move(for_sibling, 0, to_sibling)
    outer = move(for_outer, 0, to_outer)
    pouter = move(for_outer, 1, to_outer)
    (
        wcur, wear, wboth, w2own, w2first, w2rest, w2b, w2brest, wgear, wgcur, wgboth, bias,
    ) = weights(first_kernel, second_kernel, first_bias[None])
    xd, icur, ihown, itown = own_inner(wide, wcur, wboth, bias, w2own)
    rcur, rhown, rtown, rcot = own_rim(
        sibling, outer, cot16, xd, wcur, wboth, bias, w2own
    )
    prev, rcur, pouter = lax.optimization_barrier((prev, rcur, pouter))
    psib = move(prev, 0, to_sibling)
    ilow, xp, ihmid, itsum, ig3, ivotes, idlow = middle(
        prev, icur, itown, cot16, consts, wear, w2first, w2rest, w2b, w2brest, wgear
    )
    iback = move(ilow, -1, same)
    rlow, rhmid, rg3, rvotes = borrowed(
        psib, pouter, xp, rcur, rtown, itsum, ihmid, ig3, idlow, rcot, consts,
        wear, w2first, w2rest, w2b, w2brest, wgear,
    )
    rback = move(rlow, -1, same)
    voted, grad = own_grad(
        ivotes, rvotes, ig3, rg3, ihown, rhown, ihmid, rhmid, w2b, wgcur, wgboth
    )
    return (voted, finish(grad, iback, rback))


def solution(mesh):
    return jax.shard_map(
        body,
        mesh=mesh,
        in_specs=(
            P("sec", None, "tile", None),
            P("sec", None, "tile", None),
            P("sec"),
            P("sec"),
            P(),
            P(),
            P(),
            P(),
        ),
        out_specs=(P("sec", None, "tile", None), P("sec", None, "tile", None)),
        check_vma=False,
    )
```

```python
import jax
import jax.numpy as jnp
from jax import lax
from jax.experimental import pallas as pl
from jax.experimental.pallas import tpu as pltpu
from jax.sharding import PartitionSpec as P

F32 = jnp.float32
BF16 = jnp.bfloat16
OWN = 3
CH = 32
HID = 64
TR = 16
COLS = 128
HALO = 4
FEAT_ROWS = TR + 2 * HALO
HID_ROWS = FEAT_ROWS - 2
FLD_ROWS = FEAT_ROWS - 4
DH_ROWS = FEAT_ROWS - 6
EDGE = HALO * OWN * CH
EDGE_ALL = EDGE + 32


def lane(shape):
    return lax.broadcasted_iota(jnp.int32, shape, len(shape) - 1)


def from_left(x):
    return jnp.where(lane(x.shape) == 0, 0.0, pltpu.roll(x, 1, x.ndim - 1))


def from_right(x):
    return jnp.where(lane(x.shape) == COLS - 1, 0.0, pltpu.roll(x, COLS - 1, x.ndim - 1))


def dot(a, b):
    return jnp.dot(a, b, preferred_element_type=F32)


def params(mib):
    return pltpu.CompilerParams(vmem_limit_bytes=mib << 20)


COST = {
    "own_rim": 0,
    "edges": 0,
    "weights": 0,
    "own_inner": 0,
    "middle": 2306,
    "borrowed": 3459,
    "own_grad": 3459,
    "finish": 1153,
}
INNER = TR - 2
RIM = HID_ROWS - INNER
INNER_PAIRS = [HALO + 2 * i for i in range(INNER // 2)]
RIM_PAIRS = [0, 2, HALO + INNER, HALO + INNER + 2]
FLD_INNER = FLD_ROWS - 2 * HALO
DH_INNER = DH_ROWS - 2 * HALO
OUT_INNER = TR - 2 * HALO


def inner_rows(count, step=1):
    return range(HALO, HALO + count, step)


def rim_rows(count, step=1):
    return [*range(0, HALO, step), *range(HALO + count, 2 * HALO + count, step)]


def call(kernel, outs, scratch, mib, name, specs, *args):
    space = {"v": pltpu.VMEM, "h": pltpu.HBM}
    args = [
        pltpu.with_memory_space_constraint(x, pltpu.HBM) if c == "h" else x
        for x, c in zip(args, specs, strict=True)
    ]
    return pl.pallas_call(
        kernel,
        out_shape=tuple(jax.ShapeDtypeStruct(shape, kind) for shape, kind in outs),
        in_specs=[pl.BlockSpec(memory_space=space[c]) for c in specs],
        out_specs=(pl.BlockSpec(memory_space=pltpu.VMEM),) * len(outs),
        scratch_shapes=[
            item[0](item[1], item[2]) if len(item) == 3 else pltpu.VMEM(*item) for item in scratch
        ],
        compiler_params=params(mib),
        cost_estimate=pl.CostEstimate(
            flops=COST[name] * 10**6, bytes_accessed=0, transcendentals=0
        ),
        name=name,
    )(*args)


def sems(shape, _):
    return pltpu.SemaphoreType.DMA(shape)


def fetch(sems, *moves):
    copies = [pltpu.make_async_copy(a, b, sems.at[i]) for i, (a, b) in enumerate(moves)]
    for c in copies:
        c.start()
    for c in copies:
        c.wait()


def odd_tile():
    return lax.axis_index("tile") % 2 == 1


def has_tiles():
    tile = lax.axis_index("tile")
    return (tile > 0).astype(F32), (tile < lax.axis_size("tile") - 1).astype(F32)


class Rows:
    def __init__(self, inner, rim, count=INNER):
        self.inner, self.rim, self.count = inner, rim, count

    def at(self, r):
        if r < HALO:
            return self.rim, r
        if r < HALO + self.count:
            return self.inner, r - HALO
        return self.rim, r - self.count

    def pair(self, r, first, n):
        ref, i = self.at(r)
        return pair_row(ref, i, first, n)

    def put(self, r, first, x):
        ref, i = self.at(r)
        halves(ref, i, first, x)


def edges_kernel(
    valid_hbm, sharp_hbm, b2_hbm, feat_hbm, vgrad_hbm,
    sibling, outer, wide, cot, consts,
    valid, sharp, b2, feat, vgrad, ext, sems,
):
    fetch(
        sems,
        (feat_hbm, feat), (vgrad_hbm, vgrad), (valid_hbm, valid), (sharp_hbm, sharp), (b2_hbm, b2),
    )
    row0 = lax.axis_index("tile") * TR
    odd = odd_tile()
    for s in range(OWN):
        wide[s] = feat[s].astype(F32)
        pos = row0 + lax.broadcasted_iota(jnp.int32, (TR, COLS), 0)
        for c in range(2):
            cot[s, c] = jnp.where(pos < valid[s], vgrad[s, c], 0.0)
        consts[s] = jnp.full((8, COLS), sharp[s], F32)
    even_row = lax.broadcasted_iota(jnp.int32, (8, COLS), 0) % 2 == 0
    consts[OWN] = jnp.where(even_row, b2[0], b2[1])
    for out, last in ((sibling, jnp.logical_not(odd)), (outer, odd)):
        ext[...] = jnp.zeros((32, COLS), F32)
        for s in range(OWN):
            for c in range(2):
                x = jnp.where(last, cot[s, c, TR - 2 :, :], cot[s, c, 0:2, :])
                high = x.astype(BF16).astype(F32)
                at = s * 4 + c * 2
                ext[at : at + 2, :] = high
                ext[12 + at : 14 + at, :] = x - high
        out[EDGE:, :] = ext[...].astype(BF16)
        for s in range(OWN):
            for r in range(HALO):
                at = (r * OWN + s) * CH
                x = jnp.where(last, wide[s, :, TR - HALO + r, :], wide[s, :, r, :])
                out[at : at + CH, :] = x.astype(BF16)


def edges(*args):
    return call(
        edges_kernel,
        [
            ((EDGE_ALL, COLS), BF16),
            ((EDGE_ALL, COLS), BF16),
            ((OWN, CH, TR, COLS), F32),
            ((OWN, 2, TR, COLS), F32),
            ((OWN + 1, 8, COLS), F32),
        ],
        [
            (pltpu.SMEM, (OWN,), jnp.int32),
            (pltpu.SMEM, (OWN,), F32),
            (pltpu.SMEM, (2,), F32),
            ((OWN, CH, TR, COLS), BF16),
            ((OWN, 2, TR, COLS), F32),
            ((32, COLS), F32),
            (sems, (5,), None),
        ],
        3,
        "edges",
        "hhhhh",
        *args,
    )


def weights_kernel(
    k1_hbm, k2_hbm, b1_hbm, wcur, wear, wboth, w2own, w2first, w2rest, w2b, w2brest, wgear, wgcur, wgboth, bias,
    k1, k2, b1, fwd, bwd, both, two, sq, sems,
):
    fetch(sems, (k1_hbm, k1), (k2_hbm, k2), (b1_hbm, b1))
    bias[...] = jnp.broadcast_to(b1[...], (COLS, HID)).T
    for dy in range(3):
        for dx in range(3):
            k = k1[dy, dx].astype(F32)
            t = CH * (3 * dy + dx)
            fwd[0:HID, t : t + CH] = k[:, :CH]
            fwd[HID:, t : t + CH] = k[:, CH:]
            kt = k.T
            rows = slice(CH * dx, CH * dx + CH)
            bwd[rows, HID * dy : HID * dy + HID] = kt[:CH]
            bwd[3 * CH + CH * dx : 4 * CH + CH * dx, HID * dy : HID * dy + HID] = kt[CH:]
            both[rows, 2 * HID * dy : 2 * HID * dy + HID] = kt[:CH]
            both[rows, 2 * HID * dy + HID : 2 * HID * dy + 2 * HID] = kt[CH:]
    wcur[...] = fwd[0:HID, :].astype(BF16)
    wear[...] = fwd[HID:, :].astype(BF16)
    wboth[...] = fwd[...].astype(BF16)
    wgcur[...] = bwd[0 : 3 * CH, :].astype(BF16)
    wgear[...] = bwd[3 * CH :, :].astype(BF16)
    wgboth[...] = both[...].astype(BF16)

    def put(ref, row, col, lags):
        for i, lag in enumerate(lags):
            for dy in range(3):
                for dx in range(3):
                    at = row + 8 * (3 * dy + dx) + 2 * lag
                    c = col + HID * i
                    ref[at : at + 2, c : c + HID] = k2[dy, dx].astype(F32)

    two[...] = jnp.zeros(two.shape, F32)
    put(two, 0, 0, (0, 1, 2))
    w2first[...] = two[0:72, :].astype(BF16)
    two[...] = jnp.zeros(two.shape, F32)
    put(two, 0, 0, (1, 2))
    put(two, 72, 2 * HID, (2,))
    w2rest[...] = two[...].astype(BF16)
    two[...] = jnp.zeros(two.shape, F32)
    put(two, 0, 0, (0,))
    put(two, 72, HID, (0, 1))
    w2own[...] = two[...].astype(BF16)

    def lay(row, col, lags):
        for i, lag in enumerate(lags):
            for dy in range(3):
                for dx in range(3):
                    at = row + 32 * dy + 8 * dx + 2 * lag
                    c = col + HID * i
                    sq[at : at + 2, c : c + HID] = k2[dy, dx].astype(F32)

    sq[...] = jnp.zeros(sq.shape, F32)
    lay(0, 0, (0, 1, 2))
    w2b[...] = sq[0:96, :].T.astype(BF16)
    sq[...] = jnp.zeros(sq.shape, F32)
    lay(0, 0, (1, 2))
    lay(96, 2 * HID, (2,))
    w2brest[...] = sq[...].T.astype(BF16)


def weights(k1, k2, b1):
    return call(
        weights_kernel,
        [
            ((HID, 9 * CH), BF16),
            ((HID, 9 * CH), BF16),
            ((2 * HID, 9 * CH), BF16),
            ((144, 192), BF16),
            ((72, 192), BF16),
            ((144, 192), BF16),
            ((192, 96), BF16),
            ((192, 192), BF16),
            ((3 * CH, 3 * HID), BF16),
            ((3 * CH, 3 * HID), BF16),
            ((3 * CH, 6 * HID), BF16),
            ((HID, COLS), F32),
        ],
        [
            (k1.shape, BF16),
            (k2.shape, BF16),
            (b1.shape, F32),
            ((2 * HID, 9 * CH), F32),
            ((6 * CH, 3 * HID), F32),
            ((3 * CH, 6 * HID), F32),
            ((144, 192), F32),
            ((192, 192), F32),
            (sems, (3,), None),
        ],
        4,
        "weights",
        "hhh",
        k1,
        k2,
        b1,
    )


def spread_row(x, xd, j, r):
    xd[j, r, 0:CH, :] = from_left(x).astype(BF16)
    xd[j, r, CH : 2 * CH, :] = x.astype(BF16)
    xd[j, r, 2 * CH :, :] = from_right(x).astype(BF16)


def spread_own(wide, keep, xd):
    for s in range(OWN):
        for r in range(TR):
            x = wide[s, :, r, :]
            spread_row(x if keep is None else x * keep, xd, s, r)


def spread_rim(pick, scale, xr):
    for s in range(OWN):
        for r in range(HALO):
            for side in range(2):
                spread_row(pick(side, s, r) * scale[side], xr, s, HALO * side + r)


def feature_rows(xd, xr):
    def pick(j, r):
        if r < HALO:
            return xr[j, r]
        if r < HALO + TR:
            return xd[j, r - HALO]
        return xr[j, r - TR]

    return pick


def taps(rows, pick):
    return jnp.concatenate(
        [jnp.concatenate([pick(r), pick(r + 1)], axis=1) for r in rows], axis=0
    )


def halves(ref, r, first, x):
    n = x.shape[0]
    ref[r, first : first + n, :] = x[:, :COLS]
    ref[r + 1, first : first + n, :] = x[:, COLS:]


def pair_row(ref, r, first, n):
    return jnp.concatenate(
        [ref[r, first : first + n, :], ref[r + 1, first : first + n, :]], axis=1
    )


def gather_columns(p):
    return from_right(p[:CH]) + p[CH : 2 * CH] + from_left(p[2 * CH :])


def hidden_own(pairs, pick, wcur, wboth, bias, w2own, cur, hown, town):
    b = jnp.concatenate([bias[...], bias[...]], axis=1)
    for r in pairs:
        rhs = [taps((r, r + 1, r + 2), lambda q, j=j: pick(j, q)) for j in range(OWN)]
        both = [dot(wboth[...], rhs[j]) for j in range(2)]
        c = [both[0][:HID] + b, both[1][:HID] + b, dot(wcur[...], rhs[2]) + b]
        ear = [both[0][HID:], both[1][HID:]]
        for s in range(OWN):
            cur.put(r, HID * s, c[s])
        h = jnp.concatenate(
            [jnp.maximum(x, 0.0) for x in (c[1] + ear[0], c[2] + ear[1], c[2] + ear[0])], axis=0
        ).astype(BF16)
        hown.put(r, 0, h)
        town.put(r, 0, dot(w2own[...], h))


def hidden_borrowed(pairs, pick, wear, w2first, w2rest, cur, town, hmid, tsum):
    for r in pairs:
        ear = [
            dot(wear[...], taps((r, r + 1, r + 2), lambda q, j=j: pick(j, q)))
            for j in range(OWN)
        ]
        c = [cur.pair(r, HID * s, HID) for s in range(OWN)]
        h = [
            jnp.concatenate([jnp.maximum(c[s] + ear[3 + s - k], 0.0) for s, k in part], axis=0)
            for part in (((0, 1), (0, 2), (0, 3)), ((1, 2), (1, 3), (2, 3)))
        ]
        h = [x.astype(BF16) for x in h]
        hmid.put(r, 0, h[0])
        hmid.put(r, 192, h[1])
        tsum.put(r, 0, dot(w2first[...], h[0]))
        tsum.put(r, 72, dot(w2rest[...], h[1]) + town.pair(r, 0, 144))


def own_kernel(wide, wcur, wboth, bias, w2own, xd, cur, hown, town):
    spread_own(wide, None, xd)
    hidden_own(
        INNER_PAIRS, feature_rows(xd, None), wcur, wboth, bias, w2own,
        Rows(cur, None), Rows(hown, None), Rows(town, None),
    )


def hidden_outs(n):
    return [
        ((n, OWN * HID, COLS), F32),
        ((n, 3 * HID, COLS), BF16),
        ((n, 144, COLS), F32),
    ]


def own_inner(*args):
    return call(
        own_kernel,
        [((OWN, TR, 3 * CH, COLS), BF16)] + hidden_outs(INNER),
        [],
        2,
        "own_inner",
        "v" * len(args),
        *args,
    )


def rim_kernel(
    sibling, outer, cot16, xd, wcur, wboth, bias, w2own, rcur, rhown, rtown, rcot, xr
):
    odd = odd_tile()
    has = has_tiles()

    def halo(side, first, n):
        x, y = sibling[first : first + n, :], outer[first : first + n, :]
        x, y = x.astype(F32), y.astype(F32)
        return jnp.where(odd, x, y) if side == 0 else jnp.where(odd, y, x)

    for side, first in ((0, 0), (1, 6)):
        ext = halo(side, EDGE, 32) * has[side]
        for s in range(OWN):
            for c in range(2):
                at = s * 4 + c * 2
                rcot[s, c, first : first + 2, :] = ext[at : at + 2] + ext[12 + at : 14 + at]
    for s in range(OWN):
        for c in range(2):
            rcot[s, c, 2:4, :] = cot16[s, c, 0:2, :]
            rcot[s, c, 4:6, :] = cot16[s, c, TR - 2 :, :]
    spread_rim(lambda side, s, r: halo(side, (r * OWN + s) * CH, CH), has, xr)
    hidden_own(
        RIM_PAIRS, feature_rows(xd, xr), wcur, wboth, bias, w2own,
        Rows(None, rcur), Rows(None, rhown), Rows(None, rtown),
    )


def own_rim(*args):
    return call(
        rim_kernel,
        hidden_outs(RIM) + [((OWN, 2, 8, COLS), F32)],
        [((OWN, 2 * HALO, 3 * CH, COLS), BF16)],
        2,
        "own_rim",
        "v" * len(args),
        *args,
    )


def middle_kernel(
    prev, icur, itown, cot16, consts, wear, w2first, w2rest, w2b, w2brest, wgear,
    low, xp, ihmid, itsum, ig3, ivotes, idlow,
    wide, fld, grd,
):
    keep = (lax.axis_index("sec") > 0).astype(F32)
    for s in range(OWN):
        wide[s] = prev[s].astype(F32)
    spread_own(wide, keep, xp)
    hmid, tsum = Rows(ihmid, None), Rows(itsum, None)
    hidden_borrowed(
        INNER_PAIRS, feature_rows(xp, None), wear, w2first, w2rest,
        Rows(icur, None), Rows(itown, None), hmid, tsum,
    )
    fields_stage(inner_rows(FLD_INNER), tsum, consts.at[OWN], None, fld)
    vote_stage(
        FLD_INNER, consts, lambda s, c: cot16[s, c, 2 : TR - 2, :], fld, grd, ig3, ivotes
    )
    dlow = Rows(idlow, None, DH_INNER)
    low_grad_stage(
        inner_rows(DH_INNER, 2), w2b, w2brest, grad_rows(ig3, None), hmid, dlow
    )
    low_stage(inner_rows(OUT_INNER, 2), wgear, dlow, Rows(low, None, OUT_INNER))


def middle(*args):
    return call(
        middle_kernel,
        [
            ((OUT_INNER, OWN, CH, COLS), BF16),
            ((OWN, TR, 3 * CH, COLS), BF16),
            ((INNER, 6 * HID, COLS), BF16),
            ((INNER, OWN * 72, COLS), F32),
            ((OWN, FLD_INNER, 32, COLS), BF16),
            ((OWN, 2, 16, COLS), F32),
            ((DH_INNER, 3 * HID, COLS), BF16),
        ],
        [
            ((OWN, CH, TR, COLS), F32),
            ((OWN, FLD_INNER, 8, COLS), F32),
            ((OWN, FLD_INNER, 8, COLS), F32),
        ],
        4,
        "middle",
        "v" * len(args),
        *args,
    )


def fields_stage(rows, tsum, bias2, has, fld):
    for i, r in enumerate(rows):
        for s in range(OWN):
            sums = []
            for dx in range(3):
                terms = []
                for dy in range(3):
                    at = 72 * s + 8 * (3 * dy + dx)
                    ref, j = tsum.at(r + dy)
                    t = ref[j, at : at + 8, :]
                    if r + dy < 3:
                        t = t * has[0]
                    elif r + dy > HID_ROWS - 4:
                        t = t * has[1]
                    terms.append(t)
                sums.append(terms[0] + terms[1] + terms[2])
            fld[s, i] = (sums[1] + bias2[...]) + (from_left(sums[0]) + from_right(sums[2]))


def vote_stage(n, consts, cot_of, fld, grd, g3, votes):
    for s in range(OWN):
        f = [[fld[s, :, 2 * k + c, :] for c in range(2)] for k in range(3)]
        beta = consts[s, 0:1, :]
        diff = {}
        dist = {}
        for a, b in ((0, 1), (0, 2), (1, 2)):
            diff[a, b] = [f[a][c] - f[b][c] for c in range(2)]
            dist[a, b] = diff[a, b][0] * diff[a, b][0] + diff[a, b][1] * diff[a, b][1]
        score = [dist[0, 1] + dist[0, 2], dist[0, 1] + dist[1, 2], dist[0, 2] + dist[1, 2]]
        logit = [-beta * q for q in score]
        top = jnp.maximum(jnp.maximum(logit[0], logit[1]), logit[2])
        expo = [jnp.exp(q - top) for q in logit]
        inv = 1.0 / (expo[0] + expo[1] + expo[2])
        w = [q * inv for q in expo]
        v = [w[0] * f[0][c] + w[1] * f[1][c] + w[2] * f[2][c] for c in range(2)]
        for c in range(2):
            votes[s, c, 0:n, :] = v[c]
        g = [cot_of(s, c) for c in range(2)]
        e = [
            -beta * w[k] * (g[0] * (f[k][0] - v[0]) + g[1] * (f[k][1] - v[1])) for k in range(3)
        ]
        pair = {key: 2.0 * (e[key[0]] + e[key[1]]) for key in diff}
        for c in range(2):
            m01 = pair[0, 1] * diff[0, 1][c]
            m02 = pair[0, 2] * diff[0, 2][c]
            m12 = pair[1, 2] * diff[1, 2][c]
            grd[s, :, 0 + c, :] = w[0] * g[c] + m01 + m02
            grd[s, :, 2 + c, :] = w[1] * g[c] - m01 + m12
            grd[s, :, 4 + c, :] = w[2] * g[c] - m02 - m12
        grd[s, :, 6, :] = jnp.zeros((n, COLS), F32)
        grd[s, :, 7, :] = jnp.zeros((n, COLS), F32)
    for r in range(n):
        for s in range(OWN):
            x = grd[s, r]
            g3[s, r] = jnp.concatenate(
                [from_right(x), x, from_left(x), jnp.zeros_like(x)], axis=0
            ).astype(BF16)


def inside(ref, has):
    for r, h in ((0, has[0]), (ref.shape[0] - 1, has[1])):
        ref[r] = (ref[r].astype(F32) * h).astype(BF16)


def low_grad_stage(rows, w2b, w2brest, g3, hmid, dlow):
    for q in rows:
        rhs = [taps((q + 2, q + 1, q), lambda r, s=s: g3(s, r)) for s in range(OWN)]
        h = [hmid.pair(q + 2, 192 * j, 192).astype(F32) for j in range(2)]
        first = jnp.where(h[0] > 0.0, dot(w2b[...], rhs[0]), 0.0)
        rest = jnp.where(
            h[1] > 0.0, dot(w2brest[...], jnp.concatenate([rhs[1], rhs[2]], axis=0)), 0.0
        )
        low = jnp.concatenate(
            [
                first[2 * HID :],
                first[HID : 2 * HID] + rest[HID : 2 * HID],
                first[:HID] + rest[:HID] + rest[2 * HID :],
            ],
            axis=0,
        ).astype(BF16)
        dlow.put(q, 0, low)


def low_stage(rows, wgear, dlow, low):
    for r in rows:
        for s in range(OWN):

            def pick(q, s=s):
                ref, i = dlow.at(q)
                return ref[i, HID * s : HID * s + HID, :]

            p = dot(wgear[...], taps((r + 2, r + 1, r), pick))
            for d in range(2):
                ref, i = low.at(r + d)
                ref[i, s] = gather_columns(p[:, COLS * d : COLS * d + COLS]).astype(BF16)


def grad_rows(ig3, rg3):
    rows = Rows(ig3, rg3, FLD_INNER)

    def pick(s, r):
        ref, i = rows.at(r)
        return ref[s, i]

    return pick


def feature_grad_stage(dref, jobs, unroll):
    def step(i, carry):
        r = 2 * i
        for first, size, weight, out, s in jobs:
            rhs = taps((r + 2, r + 1, r), lambda q: dref[q, first : first + size, :])
            p = dot(weight[...], rhs)
            for d in range(2):
                out[r + d, s] = gather_columns(p[:, COLS * d : COLS * d + COLS]).astype(out.dtype)
        return carry

    lax.fori_loop(0, TR // 2, step, 0, unroll=unroll)


def borrowed_kernel(
    psib, pouter, xp, rcur, rtown, itsum, ihmid, ig3, idlow, rcot, consts,
    wear, w2first, w2rest, w2b, w2brest, wgear,
    low, rhmid, rg3, rvotes,
    wide, xr, rtsum, fld, grd, rdlow,
):
    odd = odd_tile()
    has = has_tiles()
    keep = (lax.axis_index("sec") > 0).astype(F32)
    for s in range(OWN):
        wide[s] = psib[s].astype(F32)

    def halo(side, s, r):
        at = (r * OWN + s) * CH
        y = pouter[at : at + CH, :].astype(F32)
        if side == 0:
            return jnp.where(odd, wide[s, :, TR - HALO + r, :], y)
        return jnp.where(odd, y, wide[s, :, r, :])

    spread_rim(halo, [keep * h for h in has], xr)
    hmid, tsum = Rows(ihmid, rhmid), Rows(itsum, rtsum)
    hidden_borrowed(
        RIM_PAIRS, feature_rows(xp, xr), wear, w2first, w2rest,
        Rows(None, rcur), Rows(None, rtown), hmid, tsum,
    )
    fields_stage(rim_rows(FLD_INNER), tsum, consts.at[OWN], has, fld)
    vote_stage(2 * HALO, consts, lambda s, c: rcot[s, c], fld, grd, rg3, rvotes)
    dlow = Rows(idlow, rdlow, DH_INNER)
    low_grad_stage(rim_rows(DH_INNER, 2), w2b, w2brest, grad_rows(ig3, rg3), hmid, dlow)
    inside(rdlow, has)
    low_stage(rim_rows(OUT_INNER, 2), wgear, dlow, Rows(None, low, OUT_INNER))


def borrowed(*args):
    return call(
        borrowed_kernel,
        [
            ((2 * HALO, OWN, CH, COLS), BF16),
            ((RIM, 6 * HID, COLS), BF16),
            ((OWN, 2 * HALO, 32, COLS), BF16),
            ((OWN, 2, 8, COLS), F32),
        ],
        [
            ((OWN, CH, TR, COLS), F32),
            ((OWN, 2 * HALO, 3 * CH, COLS), BF16),
            ((RIM, OWN * 72, COLS), F32),
            ((OWN, 2 * HALO, 8, COLS), F32),
            ((OWN, 2 * HALO, 8, COLS), F32),
            ((2 * HALO, 3 * HID, COLS), BF16),
        ],
        6,
        "borrowed",
        "v" * len(args),
        *args,
    )


def own_grad_kernel(
    ivotes, rvotes, ig3, rg3, ihown, rhown, ihmid, rhmid, w2b, wgcur, wgboth, voted, grad, down
):
    has = has_tiles()
    hown, hmid = Rows(ihown, rhown), Rows(ihmid, rhmid)
    g3 = grad_rows(ig3, rg3)
    for s in range(OWN):
        for c in range(2):
            voted[s, c, 0:2, :] = rvotes[s, c, 2:4, :]
            voted[s, c, 2 : TR - 2, :] = ivotes[s, c, 0:FLD_INNER, :]
            voted[s, c, TR - 2 :, :] = rvotes[s, c, 4:6, :]
    for q in range(0, DH_ROWS, 2):
        ho = hown.pair(q + 2, 0, 192)
        hm = hmid.pair(q + 2, 0, 384)
        h = [
            hm[:192],
            jnp.concatenate([ho[:64], hm[192:320]], axis=0),
            jnp.concatenate([ho[64:], hm[320:]], axis=0),
        ]
        m = []
        for s in range(OWN):
            dh = dot(w2b[...], taps((q + 2, q + 1, q), lambda r, s=s: g3(s, r)))
            dh = jnp.where(h[s].astype(F32) > 0.0, dh, 0.0)
            m.append([dh[HID * k : HID * k + HID] for k in range(3)])
        c = [m[s][0] + m[s][1] + m[s][2] for s in range(OWN)]
        d = jnp.concatenate([c[0], m[1][0] + m[2][1], c[1], m[2][0], c[2]], axis=0).astype(BF16)
        halves(down, q, 0, d)
    inside(down, has)
    feature_grad_stage(
        down,
        [(0, 128, wgboth, grad, 0), (128, 128, wgboth, grad, 1), (256, 64, wgcur, grad, 2)],
        4,
    )


def own_grad(*args):
    return call(
        own_grad_kernel,
        [((OWN, 2, TR, COLS), F32), ((TR, OWN, CH, COLS), F32)],
        [((DH_ROWS, 5 * HID, COLS), BF16)],
        4,
        "own_grad",
        "v" * len(args),
        *args,
    )


def finish_kernel(grad, iback, rback, out, block, sems):
    keep = (lax.axis_index("sec") < lax.axis_size("sec") - 1).astype(F32)
    back = Rows(iback, rback, OUT_INNER)
    copies = []
    for s in range(OWN):
        for r in range(TR):
            ref, i = back.at(r)
            block[s, :, r, :] = grad[r, s] + ref[i, s].astype(F32) * keep
        copies.append(pltpu.make_async_copy(block.at[s], out.at[s], sems.at[s]))
        copies[-1].start()
    for c in copies:
        c.wait()


def finish(*args):
    vmem = pl.BlockSpec(memory_space=pltpu.VMEM)
    return pl.pallas_call(
        finish_kernel,
        out_shape=jax.ShapeDtypeStruct((OWN, CH, TR, COLS), F32),
        in_specs=[vmem] * len(args),
        out_specs=pl.BlockSpec(memory_space=pltpu.HBM),
        scratch_shapes=[
            pltpu.VMEM((OWN, CH, TR, COLS), F32),
            pltpu.SemaphoreType.DMA((OWN,)),
        ],
        compiler_params=params(2),
        name="finish",
    )(*args)


def move(value, secs, tile_to):
    n, m = lax.axis_size("sec"), lax.axis_size("tile")
    pairs = []
    for a in range(n):
        for b in range(m):
            to = tile_to(b)
            pairs.append((a * m + b, a * m + b if to is None else ((a + secs) % n) * m + to))
    return lax.ppermute(value, ("sec", "tile"), pairs)


def body(
    features, vote_grad, sharpness, valid_rows, first_kernel, first_bias, second_kernel, second_bias
):
    tiles = lax.axis_size("tile")

    def same(b):
        return b

    def to_sibling(b):
        return b + 1 - 2 * (b % 2)

    def to_outer(b):
        other = b - 1 + 2 * (b % 2)
        return other if 0 <= other < tiles else None

    prev = move(features, 1, same)
    for_sibling, for_outer, wide, cot16, consts = edges(
        valid_rows, sharpness, second_bias, features, vote_grad
    )
    sibling = move(for_sibling, 0, to_sibling)
    outer = move(for_outer, 0, to_outer)
    pouter = move(for_outer, 1, to_outer)
    (
        wcur, wear, wboth, w2own, w2first, w2rest, w2b, w2brest, wgear, wgcur, wgboth, bias,
    ) = weights(first_kernel, second_kernel, first_bias[None])
    xd, icur, ihown, itown = own_inner(wide, wcur, wboth, bias, w2own)
    rcur, rhown, rtown, rcot = own_rim(
        sibling, outer, cot16, xd, wcur, wboth, bias, w2own
    )
    prev, rcur, pouter = lax.optimization_barrier((prev, rcur, pouter))
    psib = move(prev, 0, to_sibling)
    ilow, xp, ihmid, itsum, ig3, ivotes, idlow = middle(
        prev, icur, itown, cot16, consts, wear, w2first, w2rest, w2b, w2brest, wgear
    )
    iback = move(ilow, -1, same)
    rlow, rhmid, rg3, rvotes = borrowed(
        psib, pouter, xp, rcur, rtown, itsum, ihmid, ig3, idlow, rcot, consts,
        wear, w2first, w2rest, w2b, w2brest, wgear,
    )
    rback = move(rlow, -1, same)
    voted, grad = own_grad(
        ivotes, rvotes, ig3, rg3, ihown, rhown, ihmid, rhmid, w2b, wgcur, wgboth
    )
    return (voted, finish(grad, iback, rback))


def solution(mesh):
    return jax.shard_map(
        body,
        mesh=mesh,
        in_specs=(
            P("sec", None, "tile", None),
            P("sec", None, "tile", None),
            P("sec"),
            P("sec"),
            P(),
            P(),
            P(),
            P(),
        ),
        out_specs=(P("sec", None, "tile", None), P("sec", None, "tile", None)),
        check_vma=False,
    )
```
